32 devices in a mesh: ctx: 8 (over z, y), head: 4 (over x, core).
Axes of the slice: x: 2, y: 2, z: 4, core: 2. Of those that a mesh axis runs over, the one named last changes fastest.
Arguments:
- queries: bfloat16 [2048, 2048], P('ctx', 'head'), may hold values from -6 to 6
- keys: bfloat16 [2048, 2048], P('ctx', 'head'), may hold values from -6 to 6
- values: bfloat16 [2048, 2048], P('ctx', 'head'), may hold values from -6 to 6
- out_grad: bfloat16 [2048, 2048], P('ctx', 'head'), may hold values from -6 to 6
- doc_lengths: int32 [8], replicated, may hold values from 1 to 768, as said below
Outputs:
- attended: float32 [2048, 2048], P('ctx', 'head')
- query_grad: float32 [2048, 2048], P('ctx', 'head')
- key_grad: float32 [2048, 2048], P('ctx', 'head')
- value_grad: float32 [2048, 2048], P('ctx', 'head')
The draws below stay inside these ranges and needn't reach their ends.
Inputs may be any that keep to these rules, and one draw needn't show every extreme that they name: `doc_lengths`: the first document has exactly 768 tokens, every other one 1 to 768, and all lengths sum to 2048.
All inputs are finite; a program needn't handle non-finite values.
Results may differ from the reference program's by a relative error of at most 0.0095.
Values may be sent and summed in bfloat16 or wider, within the bound.
A program may use at most 64 MiB of HBM per device.

```python
import jax
import jax.numpy as jnp
from jax import lax

HEADS = 16
HD = 128
TOK_DEV = 256
TOKENS = 2048
PROMPT = 64
SPAN = 3
DOC_MOST = 768
DOCS = 8
N_CTX = 8


def draw_queries(key, part):
    key = jax.random.fold_in(key, 1)
    drawn = jnp.clip(jax.random.normal(key, (TOKENS, HEADS * HD), jnp.float32), -6.0, 6.0)
    return drawn.astype(jnp.bfloat16)


def draw_keys(key, part):
    key = jax.random.fold_in(key, 2)
    drawn = jnp.clip(jax.random.normal(key, (TOKENS, HEADS * HD), jnp.float32), -6.0, 6.0)
    return drawn.astype(jnp.bfloat16)


def draw_doc_lengths(key, part):
    key = jax.random.fold_in(key, 3)
    remaining = TOKENS - DOC_MOST
    others = DOCS - 1
    places = jnp.arange(others, dtype=jnp.int32)
    even_split = (places + 1) * remaining // others - places * remaining // others
    least = remaining // others
    spread = max(0, min(least - 1, DOC_MOST - least - 1) // 2)
    moves = jax.random.randint(key, (others,), -spread, spread + 1)
    lengths = even_split + moves - jnp.roll(moves, -1)
    return jnp.concatenate([jnp.full((1,), DOC_MOST, jnp.int32), lengths.astype(jnp.int32)])


def steps_of(stream_key, shape, shards, low, top_value):
    def one(axis_at, blocks):
        heights = jax.random.uniform(jax.random.fold_in(jax.random.fold_in(stream_key, 6), axis_at), (blocks,), jnp.float32, low / len(shards), top_value / len(shards))
        return jnp.repeat(jnp.exp(heights), shape[axis_at] // blocks).reshape((-1,) + (1,) * (len(shape) - axis_at - 1))

    level = one(*shards[0])
    for cut in shards[1:]:
        level = level * one(*cut)
    return level


def scatter_about(key, dims, width, most, shards=(), kind=jnp.bfloat16):
    values = jax.random.normal(key, dims, jnp.float32) * width
    if len(shards) > 0:
        values = steps_of(key, dims, shards, -0.22, 0.18) * values
    return jnp.clip(values, min=-most, max=most).astype(kind)


def setup_inputs(seed: int = 0) -> dict:
    key_of = jax.random.split(jax.random.key(seed), 6)
    queries = draw_queries(jax.random.fold_in(key_of[5], 71), 0)
    keys = draw_keys(jax.random.fold_in(key_of[5], 71), 0)
    values = scatter_about(key_of[2], (TOKENS, HEADS * HD), 1.0, 6.0, ((0, 8), (1, 4)))
    out_grad = scatter_about(key_of[3], (TOKENS, HEADS * HD), 1.0, 6.0, ((0, 8), (1, 4)))
    doc_lengths = draw_doc_lengths(jax.random.fold_in(key_of[5], 71), 0)
    return dict(queries=queries, keys=keys, values=values, out_grad=out_grad, doc_lengths=doc_lengths)


def segment_ids(doc_lengths, positions):
    doc_ends = jnp.cumsum(doc_lengths).astype(jnp.int32)
    return jnp.sum((doc_ends[None, :] <= positions[:, None]).astype(jnp.int32), axis=1).astype(jnp.int32)


def reference(queries, keys, values, out_grad, doc_lengths):
    score_scale = 1.0 / (HD ** 0.5)
    window = (SPAN + 1) * TOK_DEV
    front = SPAN * TOK_DEV
    q_all = queries.reshape(TOKENS, HEADS, HD)
    k_all = keys.reshape(TOKENS, HEADS, HD)
    v_all = values.reshape(TOKENS, HEADS, HD)
    dout_all = out_grad.reshape(TOKENS, HEADS, HD)
    k_prompt = k_all[:PROMPT]
    v_prompt = v_all[:PROMPT]
    prompt_pos = jnp.arange(PROMPT, dtype=jnp.int32)
    k_pad = jnp.concatenate([jnp.zeros((front, HEADS, HD), keys.dtype), k_all], axis=0)
    v_pad = jnp.concatenate([jnp.zeros((front, HEADS, HD), values.dtype), v_all], axis=0)
    seg_all = segment_ids(doc_lengths, jnp.arange(TOKENS, dtype=jnp.int32))
    seg_pad = jnp.concatenate([-jnp.ones((front,), jnp.int32), seg_all]).astype(jnp.int32)

    def tile_setup(index):
        start = (index * TOK_DEV).astype(jnp.int32)
        q_blk = lax.dynamic_slice_in_dim(q_all, start, TOK_DEV, 0)
        k_win = lax.dynamic_slice_in_dim(k_pad, start, window, 0)
        v_win = lax.dynamic_slice_in_dim(v_pad, start, window, 0)
        q_pos = start + jnp.arange(TOK_DEV, dtype=jnp.int32)
        k_pos = start - front + jnp.arange(window, dtype=jnp.int32)
        seg_q = lax.dynamic_slice_in_dim(seg_all, start, TOK_DEV, 0)
        seg_k = lax.dynamic_slice_in_dim(seg_pad, start, window, 0)
        win_ok = (k_pos[None, :] <= q_pos[:, None]) & (seg_q[:, None] == seg_k[None, :]) & (k_pos[None, :] >= PROMPT)
        prompt_ok = prompt_pos[None, :] <= q_pos[:, None]
        allowed = jnp.concatenate([prompt_ok, win_ok], axis=1)
        k_cat = jnp.concatenate([k_prompt, k_win], axis=0)
        v_cat = jnp.concatenate([v_prompt, v_win], axis=0)
        scores = jnp.einsum("thd,uhd->htu", q_blk.astype(jnp.float32), k_cat.astype(jnp.float32)) * score_scale
        return start, q_blk, k_cat, v_cat, allowed, scores

    def forward_block(index):
        start, q_blk, k_cat, v_cat, allowed, scores = tile_setup(index)
        masked = jnp.where(allowed[None], scores, -jnp.inf)
        row_top = jnp.max(masked, axis=2)
        totals = jnp.sum(jnp.exp(masked - row_top[:, :, None]), axis=2)
        lse = row_top + jnp.log(totals)
        probs = jnp.exp(masked - lse[:, :, None])
        out_blk = jnp.einsum("htu,uhd->thd", probs, v_cat.astype(jnp.float32), precision=lax.Precision.HIGHEST)
        return out_blk, lse

    outs, lses = lax.map(forward_block, jnp.arange(N_CTX, dtype=jnp.int32))
    attended = outs.reshape(TOKENS, HEADS * HD)

    def backward_block(carried, index):
        dk_pad, dv_pad, dk_prompt, dv_prompt = carried
        start, q_blk, k_cat, v_cat, allowed, scores = tile_setup(index)
        lse = lses[index]
        out_blk = outs[index]
        dout_blk = lax.dynamic_slice_in_dim(dout_all, start, TOK_DEV, 0)
        delta = jnp.sum(dout_blk.astype(jnp.float32) * out_blk, axis=2).T
        weights = jnp.where(allowed[None], jnp.exp(scores - lse[:, :, None]), 0.0)
        rounded = lax.optimization_barrier(weights.astype(jnp.bfloat16))
        dv_part = jnp.einsum("htu,thd->uhd", rounded.astype(jnp.float32), dout_blk.astype(jnp.float32))
        dprob = jnp.einsum("thd,uhd->htu", dout_blk.astype(jnp.float32), v_cat.astype(jnp.float32))
        dscore = lax.optimization_barrier((weights * (dprob - delta[:, :, None])).astype(jnp.bfloat16))
        dq_blk = jnp.einsum("htu,uhd->thd", dscore.astype(jnp.float32), k_cat.astype(jnp.float32)) * score_scale
        dk_part = jnp.einsum("htu,thd->uhd", dscore.astype(jnp.float32), q_blk.astype(jnp.float32))
        dk_prompt = dk_prompt + dk_part[:PROMPT]
        dv_prompt = dv_prompt + dv_part[:PROMPT]
        dk_pad = lax.dynamic_update_slice_in_dim(dk_pad, lax.dynamic_slice_in_dim(dk_pad, start, window, 0) + dk_part[PROMPT:], start, 0)
        dv_pad = lax.dynamic_update_slice_in_dim(dv_pad, lax.dynamic_slice_in_dim(dv_pad, start, window, 0) + dv_part[PROMPT:], start, 0)
        return (dk_pad, dv_pad, dk_prompt, dv_prompt), dq_blk

    zero_pad = jnp.zeros((front + TOKENS, HEADS, HD), jnp.float32)
    zero_prompt = jnp.zeros((PROMPT, HEADS, HD), jnp.float32)
    (dk_pad, dv_pad, dk_prompt, dv_prompt), dq_blocks = lax.scan(backward_block, (zero_pad, zero_pad, zero_prompt, zero_prompt), jnp.arange(N_CTX, dtype=jnp.int32))
    dk_full = dk_pad[front:]
    dv_full = dv_pad[front:]
    dk_full = jnp.concatenate([dk_full[:PROMPT] + dk_prompt, dk_full[PROMPT:]], axis=0)
    dv_full = jnp.concatenate([dv_full[:PROMPT] + dv_prompt, dv_full[PROMPT:]], axis=0)
    query_grad = dq_blocks.reshape(TOKENS, HEADS * HD)
    key_grad = (dk_full * score_scale).reshape(TOKENS, HEADS * HD)
    value_grad = dv_full.reshape(TOKENS, HEADS * HD)
    return attended, query_grad, key_grad, value_grad
```

```python
import functools
import math

import jax
import jax.numpy as jnp
from jax import lax
from jax.experimental import pallas as pl
from jax.experimental.pallas import tpu as pltpu
from jax.sharding import PartitionSpec as P

HD = 128
PROMPT = 64
DOC_MOST = 768
REACH = 3
NEG_FILL = -1e30
SCALE = 1.0 / math.sqrt(HD)
SCALE2 = SCALE * math.log2(math.e)
MESH = pl.DeviceIdType.MESH


def remote(src, dst, send_sem, recv_sem, target):
    return pltpu.make_async_remote_copy(
        src_ref=src,
        dst_ref=dst,
        send_sem=send_sem,
        recv_sem=recv_sem,
        device_id={"ctx": target},
        device_id_type=MESH,
    )


def dot_nt(a, b):
    return lax.dot_general(a, b, (((1,), (1,)), ((), ())), preferred_element_type=jnp.float32)


def dot_nn(a, b):
    return jnp.dot(a, b, preferred_element_type=jnp.float32)


def kernel(
    n, first, len_ref, q_ref, k_ref, v_ref, g_ref,
    att_ref, dq_ref, dk_ref, dv_ref,
    kv_buf, qd_buf, pr_buf, pg_out, pg_buf, ld_own, ld_buf,
    s_buf, sp_buf, top_ref, tot_ref, lse_ref, del_ref,
    kv_ss, kv_rs, qd_ss, qd_rs, ld_ss, ld_rs, pr_ss, pr_rs, pg_ss, pg_rs,
):
    rows, width = q_ref.shape
    heads = width // HD
    docs = len_ref.shape[0]
    me = lax.axis_index("ctx")
    later = n - first

    def has_before(d):
        return (me >= d) & ((me < first) | (me >= first + d))

    def has_after(d):
        return (me + d < n) & ((me + d < first) | (me >= first))

    barrier = pltpu.get_barrier_semaphore()
    for s in range(1, n):
        pl.semaphore_signal(
            barrier, inc=1, device_id={"ctx": lax.rem(me + s, n)}, device_id_type=MESH
        )
    pl.semaphore_wait(barrier, n - 1)

    chunks = ((0, PROMPT), (PROMPT, rows - PROMPT))

    def kv_copy(d, w, c):
        part = pl.ds(*chunks[c])
        src = (k_ref, v_ref)[w]
        return remote(
            src.at[part], kv_buf.at[d - 1, w, part], kv_ss.at[d - 1, w, c], kv_rs.at[d - 1, w, c],
            lax.rem(me + d, n),
        )

    def qd_copy(d, w):
        src = (q_ref, g_ref)[w]
        return remote(
            src, qd_buf.at[d - 1, w], qd_ss.at[d - 1, w], qd_rs.at[d - 1, w],
            lax.rem(me + n - d, n),
        )

    def ld_copy(d):
        return remote(
            ld_own, ld_buf.at[d - 1], ld_ss.at[d - 1], ld_rs.at[d - 1], lax.rem(me + n - d, n)
        )

    def pr_copy(src, w):
        return remote(src, pr_buf.at[w], pr_ss.at[w], pr_rs.at[w], lax.rem(me + 2, n))

    def pg_copy():
        slot = lax.rem(me + n - first, n)
        return remote(pg_out, pg_buf.at[slot], pg_ss, pg_rs.at[slot], 0)

    distances = range(1, REACH + 1)
    for c in (0, 1):
        for d in distances:
            @pl.when(has_after(d))
            def _(d=d, c=c):
                for w in (0, 1):
                    kv_copy(d, w, c).start()
    for d in distances:
        @pl.when(has_before(d))
        def _(d=d):
            for w in (0, 1):
                qd_copy(d, w).start()

    def doc_start(pos):
        start = jnp.zeros_like(pos)
        end = jnp.int32(0)
        for i in range(docs):
            end = end + len_ref[i]
            start = jnp.where(pos >= end, end, start)
        return start

    col = lax.broadcasted_iota(jnp.int32, (rows, 1), 0)
    row = lax.broadcasted_iota(jnp.int32, (1, rows), 1)
    t_col = me * rows + col
    ds_col = doc_start(t_col)

    def hs(h):
        return pl.ds(pl.multiple_of(h * HD, HD), HD)

    def row_forward(h, keys, values, mask):
        s = dot_nt(q_ref[:, hs(h)], keys) * SCALE2
        if mask is not None:
            s = jnp.where(mask, s, NEG_FILL)
        top = top_ref[h]
        fresh = jnp.maximum(top, jnp.max(s, axis=1, keepdims=True))
        fade = jnp.exp2(top - fresh)
        p = jnp.exp2(s - fresh)
        top_ref[h] = fresh
        tot_ref[h] = tot_ref[h] * fade + jnp.sum(p, axis=1, keepdims=True)
        att_ref[:, hs(h)] = att_ref[:, hs(h)] * fade + dot_nn(p.astype(jnp.bfloat16), values)
        return s

    own_mask = (row <= col) & (me * rows + row >= ds_col)

    @pl.loop(0, heads)
    def _(h):
        s = dot_nt(q_ref[:, hs(h)], k_ref[:, hs(h)]) * SCALE2
        s = jnp.where(own_mask, s, NEG_FILL)
        top = jnp.max(s, axis=1, keepdims=True)
        p = jnp.exp2(s - top)
        s_buf[0, h] = s
        top_ref[h] = top
        tot_ref[h] = jnp.sum(p, axis=1, keepdims=True)
        att_ref[:, hs(h)] = dot_nn(p.astype(jnp.bfloat16), v_ref[:, hs(h)])

    for holder in (first - 2, first - 1):
        @pl.when(me == holder)
        def _(holder=holder):
            for w in (0, 1):
                kv_copy(holder, w, 0).wait_recv()
                pr_copy(kv_buf.at[holder - 1, w, pl.ds(0, PROMPT)], w).start()

    @pl.when(me >= first)
    def _():
        for w in (0, 1):
            pr_copy(pr_buf.at[w], w).wait_recv()

        @pl.when(me + 2 < n)
        def _():
            for w in (0, 1):
                pr_copy(pr_buf.at[w], w).start()

        @pl.loop(0, heads)
        def _(h):
            sp_buf[h] = row_forward(h, pr_buf[0, :, hs(h)], pr_buf[1, :, hs(h)], None)

    for d in distances:
        @pl.when(has_before(d))
        def _(d=d):
            for w in (0, 1):
                for c in (0, 1):
                    if c == 0 and d in (first - 2, first - 1):
                        @pl.when(me != d)
                        def _(w=w):
                            kv_copy(d, w, 0).wait_recv()
                    else:
                        kv_copy(d, w, c).wait_recv()
            mask = (me - d) * rows + row >= ds_col

            @pl.loop(0, heads)
            def _(h):
                s_buf[d, h] = row_forward(
                    h, kv_buf[d - 1, 0, :, hs(h)], kv_buf[d - 1, 1, :, hs(h)], mask
                )

    @pl.loop(0, heads)
    def _(h):
        total = tot_ref[h]
        att = att_ref[:, hs(h)] / total
        att_ref[:, hs(h)] = att
        lse_ref[h] = top_ref[h] + jnp.log2(total)
        del_ref[h] = jnp.sum(att * g_ref[:, hs(h)].astype(jnp.float32), axis=1, keepdims=True)

    lane = lax.broadcasted_iota(jnp.int32, (rows, HD), 1)
    packed = jnp.zeros((rows, HD), jnp.float32)
    for h in range(heads):
        packed = jnp.where(lane == h, lse_ref[h], packed)
        packed = jnp.where(lane == heads + h, del_ref[h], packed)
    ld_own[...] = jnp.transpose(packed)[: 2 * heads]

    for d in distances:
        @pl.when(has_before(d))
        def _(d=d):
            ld_copy(d).start()

    def column(h, q, g, lse, delta, keys, values, mask):
        s = dot_nt(keys, q) * SCALE2
        if mask is not None:
            s = jnp.where(mask, s, NEG_FILL)
        p = jnp.exp2(s - lse)
        dp = dot_nt(values, g)
        ds = (p * (dp - delta)).astype(jnp.bfloat16)
        return dot_nn(ds, q), dot_nn(p.astype(jnp.bfloat16), g)

    @pl.when(me >= first)
    def _():
        @pl.loop(0, heads)
        def _(h):
            dk, dv = column(
                h, q_ref[:, hs(h)], g_ref[:, hs(h)],
                ld_own[pl.ds(h, 1)], ld_own[pl.ds(heads + h, 1)],
                pr_buf[0, :, hs(h)], pr_buf[1, :, hs(h)], None,
            )
            pg_out[0, :, hs(h)] = dk.astype(jnp.bfloat16)
            pg_out[1, :, hs(h)] = dv.astype(jnp.bfloat16)

        pg_copy().start()

    def row_backward(h, s, keys, values):
        p = jnp.exp2(s - lse_ref[h])
        dp = dot_nt(g_ref[:, hs(h)], values)
        ds = (p * (dp - del_ref[h])).astype(jnp.bfloat16)
        return dot_nn(ds, keys) * SCALE

    own_cols = (col <= row) & (me * rows + col >= doc_start(me * rows + row))

    @pl.loop(0, heads)
    def _(h):
        dq_ref[:, hs(h)] = row_backward(h, s_buf[0, h], k_ref[:, hs(h)], v_ref[:, hs(h)])
        dk, dv = column(
            h, q_ref[:, hs(h)], g_ref[:, hs(h)],
            ld_own[pl.ds(h, 1)], ld_own[pl.ds(heads + h, 1)],
            k_ref[:, hs(h)], v_ref[:, hs(h)], own_cols,
        )
        dk_ref[:, hs(h)] = dk
        dv_ref[:, hs(h)] = dv

    @pl.when(me >= first)
    def _():
        @pl.loop(0, heads)
        def _(h):
            dq_ref[:, hs(h)] += row_backward(
                h, sp_buf[h], pr_buf[0, :, hs(h)], pr_buf[1, :, hs(h)]
            )

    for d in distances:
        @pl.when(has_before(d))
        def _(d=d):
            @pl.loop(0, heads)
            def _(h):
                dq_ref[:, hs(h)] += row_backward(
                    h, s_buf[d, h], kv_buf[d - 1, 0, :, hs(h)], kv_buf[d - 1, 1, :, hs(h)]
                )

    for d in distances:
        @pl.when(has_after(d))
        def _(d=d):
            for w in (0, 1):
                qd_copy(d, w).wait_recv()
            ld_copy(d).wait_recv()
            mask = me * rows + col >= doc_start((me + d) * rows + row)

            @pl.loop(0, heads)
            def _(h):
                dk, dv = column(
                    h, qd_buf[d - 1, 0, :, hs(h)], qd_buf[d - 1, 1, :, hs(h)],
                    ld_buf[d - 1, pl.ds(h, 1)], ld_buf[d - 1, pl.ds(heads + h, 1)],
                    k_ref[:, hs(h)], v_ref[:, hs(h)], mask,
                )
                dk_ref[:, hs(h)] += dk
                dv_ref[:, hs(h)] += dv

    @pl.when(me == 0)
    def _():
        @pl.loop(0, later)
        def _(i):
            remote(pg_out, pg_buf.at[i], pg_ss, pg_rs.at[i], 0).wait_recv()
            dk_ref[pl.ds(0, PROMPT)] += pg_buf[i, 0].astype(jnp.float32)
            dv_ref[pl.ds(0, PROMPT)] += pg_buf[i, 1].astype(jnp.float32)

    dk_ref[...] = dk_ref[...] * SCALE

    for d in distances:
        @pl.when(has_after(d))
        def _(d=d):
            for w in (0, 1):
                for c in (0, 1):
                    kv_copy(d, w, c).wait_send()

        @pl.when(has_before(d))
        def _(d=d):
            for w in (0, 1):
                qd_copy(d, w).wait_send()
            ld_copy(d).wait_send()

    @pl.when((me >= first - 2) & (me + 2 < n))
    def _():
        for w in (0, 1):
            pr_copy(pr_buf.at[w], w).wait_send()

    @pl.when(me >= first)
    def _():
        pg_copy().wait_send()


def on_device(queries, keys, values, out_grad, doc_lengths):
    rows, width = queries.shape
    heads = width // HD
    n = lax.axis_size("ctx")
    first = DOC_MOST // rows
    later = n - first
    bf, f32 = jnp.bfloat16, jnp.float32
    vmem = pl.BlockSpec(memory_space=pltpu.VMEM)
    dma = pltpu.SemaphoreType.DMA
    tile = rows * rows * heads
    out = jax.ShapeDtypeStruct((rows, width), f32)
    return pl.pallas_call(
        functools.partial(kernel, n, first),
        out_shape=[out] * 4,
        in_specs=[pl.BlockSpec(memory_space=pltpu.SMEM)] + [vmem] * 4,
        out_specs=[vmem] * 4,
        scratch_shapes=[
            pltpu.VMEM((REACH, 2, rows, width), bf),
            pltpu.VMEM((REACH, 2, rows, width), bf),
            pltpu.VMEM((2, PROMPT, width), bf),
            pltpu.VMEM((2, PROMPT, width), bf),
            pltpu.VMEM((later, 2, PROMPT, width), bf),
            pltpu.VMEM((2 * heads, rows), f32),
            pltpu.VMEM((REACH, 2 * heads, rows), f32),
            pltpu.VMEM((REACH + 1, heads, rows, rows), f32),
            pltpu.VMEM((heads, rows, PROMPT), f32),
            pltpu.VMEM((heads, rows, 1), f32),
            pltpu.VMEM((heads, rows, 1), f32),
            pltpu.VMEM((heads, rows, 1), f32),
            pltpu.VMEM((heads, rows, 1), f32),
            dma((REACH, 2, 2)), dma((REACH, 2, 2)),
            dma((REACH, 2)), dma((REACH, 2)),
            dma((REACH,)), dma((REACH,)),
            dma((2,)), dma((2,)),
            dma(()), dma((later,)),
        ],
        compiler_params=pltpu.CompilerParams(
            collective_id=0, has_side_effects=True, vmem_limit_bytes=48 * 2**20
        ),
        cost_estimate=pl.CostEstimate(
            flops=2 * 8 * 4 * tile * HD, bytes_accessed=12 * rows * width, transcendentals=8 * tile
        ),
    )(doc_lengths, queries, keys, values, out_grad)


def solution(mesh):
    block = P("ctx", "head")
    return jax.shard_map(
        on_device, mesh=mesh, in_specs=(block,) * 4 + (P(),), out_specs=(block,) * 4, check_vma=False
    )
```

```python
import functools
import math

import jax
import jax.numpy as jnp
from jax import lax
from jax.experimental import pallas as pl
from jax.experimental.pallas import tpu as pltpu
from jax.sharding import PartitionSpec as P

HD = 128
PROMPT = 64
DOC_MOST = 768
REACH = 3
NEG_FILL = -1e30
SCALE = 1.0 / math.sqrt(HD)
SCALE2 = SCALE * math.log2(math.e)
MESH = pl.DeviceIdType.MESH


def remote(src, dst, send_sem, recv_sem, target):
    return pltpu.make_async_remote_copy(
        src_ref=src,
        dst_ref=dst,
        send_sem=send_sem,
        recv_sem=recv_sem,
        device_id={"ctx": target},
        device_id_type=MESH,
    )


def dot_nt(a, b):
    return lax.dot_general(a, b, (((1,), (1,)), ((), ())), preferred_element_type=jnp.float32)


def dot_nn(a, b):
    return jnp.dot(a, b, preferred_element_type=jnp.float32)


def kernel(
    n, first, far, len_ref, q_hbm, k_hbm, v_hbm, g_hbm,
    att_ref, dq_ref, dk_ref, dv_ref,
    q_ref, k_ref, v_ref, g_ref, kv_buf, qd_buf, rl_buf, pr_buf, pg_out, pg_buf, ld_own, ld_buf,
    s_buf, sp_buf, top_ref, tot_ref, lse_ref, del_ref,
    kv_ss, kv_rs, qd_ss, qd_rs, ld_ss, ld_rs, pr_ss, pr_rs, pg_ss, pg_rs, rl_ss, rl_rs, in_sem,
):
    rows, width = q_ref.shape
    heads = width // HD
    docs = len_ref.shape[0]
    me = lax.axis_index("ctx")
    later = n - first
    reach = max(far, first - 1)
    chunks = [pl.ds(c * PROMPT, PROMPT) for c in range(rows // PROMPT)]

    def has_before(d):
        near = (me >= d) & (me < first)
        return near | (me >= first + d) if d <= far else near

    def has_after(d):
        near = me + d < first
        return near | ((me >= first) & (me + d < n)) if d <= far else near

    own_copies = [
        pltpu.make_async_copy(src, dst, in_sem.at[i])
        for i, (src, dst) in enumerate(
            ((q_hbm, q_ref), (k_hbm, k_ref), (v_hbm, v_ref), (g_hbm, g_ref))
        )
    ]
    for copy in own_copies:
        copy.start()

    barrier = pltpu.get_barrier_semaphore()
    for s in range(1, n):
        pl.semaphore_signal(
            barrier, inc=1, device_id={"ctx": lax.rem(me + s, n)}, device_id_type=MESH
        )
    pl.semaphore_wait(barrier, n - 1)

    def kv_copy(d, w, c):
        src = (k_hbm, v_hbm)[w]
        return remote(
            src.at[chunks[c]], kv_buf.at[d - 1, w, chunks[c]],
            kv_ss.at[d - 1, w, c], kv_rs.at[d - 1, w, c], lax.rem(me + d, n),
        )

    def qd_copy(d, w, c):
        src = (q_hbm, g_hbm)[w]
        return remote(
            src.at[chunks[c]], qd_buf.at[d - 1, w, chunks[c]],
            qd_ss.at[d - 1, w, c], qd_rs.at[d - 1, w, c], lax.rem(me + n - d, n),
        )

    def kv_to_relay(w, c):
        src = (k_hbm, v_hbm)[w]
        return remote(
            src.at[chunks[c]], rl_buf.at[0, w, chunks[c]], kv_ss.at[0, w, c], rl_rs.at[0, w, c], first
        )

    def qd_to_relay(w, c):
        src = (q_hbm, g_hbm)[w]
        return remote(
            src.at[chunks[c]], rl_buf.at[1, w, chunks[c]], qd_ss.at[0, w, c], rl_rs.at[1, w, c], first
        )

    def kv_relayed(w, c):
        return remote(
            rl_buf.at[0, w, chunks[c]], kv_buf.at[0, w, chunks[c]],
            rl_ss.at[0, w, c], kv_rs.at[0, w, c], first - 1,
        )

    def qd_relayed(w, c):
        return remote(
            rl_buf.at[1, w, chunks[c]], qd_buf.at[0, w, chunks[c]],
            rl_ss.at[1, w, c], qd_rs.at[0, w, c], first - 2,
        )

    parts = [(w, c) for c in range(len(chunks)) for w in (0, 1)]

    def ld_copy(d):
        return remote(
            ld_own, ld_buf.at[d - 1], ld_ss.at[d - 1], ld_rs.at[d - 1], lax.rem(me + n - d, n)
        )

    def pr_copy(src, w):
        return remote(src, pr_buf.at[w], pr_ss.at[w], pr_rs.at[w], lax.rem(me + 2, n))

    def pg_copy():
        slot = lax.rem(me + n - first, n)
        return remote(pg_out, pg_buf.at[slot], pg_ss, pg_rs.at[slot], 0)

    distances = range(1, reach + 1)
    kv_direct = lambda d: has_after(d) & (me != first - 2) if d == 1 else has_after(d)
    qd_direct = lambda d: has_before(d) & (me != first - 1) if d == 1 else has_before(d)

    for d in distances:
        @pl.when(kv_direct(d))
        def _(d=d):
            for w, c in parts:
                kv_copy(d, w, c).start()

        @pl.when(qd_direct(d))
        def _(d=d):
            for w, c in parts:
                qd_copy(d, w, c).start()

    @pl.when(me == first - 2)
    def _():
        for w, c in parts:
            kv_to_relay(w, c).start()

    @pl.when(me == first - 1)
    def _():
        for w, c in parts:
            qd_to_relay(w, c).start()

    for holder in (first - 2, first - 1):
        @pl.when(me == holder)
        def _(holder=holder):
            for w in (0, 1):
                kv_copy(holder, w, 0).wait_recv()
                pr_copy(kv_buf.at[holder - 1, w, pl.ds(0, PROMPT)], w).start()

    def pass_prompt():
        for w in (0, 1):
            pr_copy(pr_buf.at[w], w).wait_recv()

            @pl.when(me + 2 < n)
            def _(w=w):
                pr_copy(pr_buf.at[w], w).start()

    @pl.when(me == first)
    def _():
        pass_prompt()
        for w, c in parts:
            remote(
                rl_buf.at[0, w, chunks[c]], rl_buf.at[0, w, chunks[c]],
                rl_ss.at[0, w, c], rl_rs.at[0, w, c], first - 1,
            ).wait_recv()
            kv_relayed(w, c).start()
            remote(
                rl_buf.at[1, w, chunks[c]], rl_buf.at[1, w, chunks[c]],
                rl_ss.at[1, w, c], rl_rs.at[1, w, c], first - 1,
            ).wait_recv()
            qd_relayed(w, c).start()

    for copy in own_copies:
        copy.wait()

    def doc_start(pos):
        start = jnp.zeros_like(pos)
        end = jnp.int32(0)
        for i in range(docs):
            end = end + len_ref[i]
            start = jnp.where(pos >= end, end, start)
        return start

    col = lax.broadcasted_iota(jnp.int32, (rows, 1), 0)
    row = lax.broadcasted_iota(jnp.int32, (1, rows), 1)
    t_col = me * rows + col
    ds_col = doc_start(t_col)

    def hs(h):
        return pl.ds(pl.multiple_of(h * HD, HD), HD)

    def row_forward(h, keys, values, mask):
        s = dot_nt(q_ref[:, hs(h)], keys) * SCALE2
        if mask is not None:
            s = jnp.where(mask, s, NEG_FILL)
        top = top_ref[h]
        fresh = jnp.maximum(top, jnp.max(s, axis=1, keepdims=True))
        fade = jnp.exp2(top - fresh)
        p = jnp.exp2(s - fresh)
        top_ref[h] = fresh
        tot_ref[h] = tot_ref[h] * fade + jnp.sum(p, axis=1, keepdims=True)
        att_ref[:, hs(h)] = att_ref[:, hs(h)] * fade + dot_nn(p.astype(jnp.bfloat16), values)
        return s

    own_mask = (row <= col) & (me * rows + row >= ds_col)

    @pl.loop(0, heads, unroll=2)
    def _(h):
        s = dot_nt(q_ref[:, hs(h)], k_ref[:, hs(h)]) * SCALE2
        s = jnp.where(own_mask, s, NEG_FILL)
        top = jnp.max(s, axis=1, keepdims=True)
        p = jnp.exp2(s - top)
        s_buf[0, h] = s
        top_ref[h] = top
        tot_ref[h] = jnp.sum(p, axis=1, keepdims=True)
        att_ref[:, hs(h)] = dot_nn(p.astype(jnp.bfloat16), v_ref[:, hs(h)])

    @pl.when(me > first)
    def _():
        pass_prompt()

    @pl.when(me >= first)
    def _():
        @pl.loop(0, heads, unroll=2)
        def _(h):
            sp_buf[h] = row_forward(h, pr_buf[0, :, hs(h)], pr_buf[1, :, hs(h)], None)

    for d in distances:
        @pl.when(has_before(d))
        def _(d=d):
            for w, c in parts:
                if c == 0 and d in (first - 2, first - 1):
                    @pl.when(me != d)
                    def _(w=w):
                        kv_copy(d, w, 0).wait_recv()
                else:
                    kv_copy(d, w, c).wait_recv()
            mask = (me - d) * rows + row >= ds_col

            @pl.loop(0, heads, unroll=2)
            def _(h):
                s_buf[d, h] = row_forward(
                    h, kv_buf[d - 1, 0, :, hs(h)], kv_buf[d - 1, 1, :, hs(h)], mask
                )

    @pl.loop(0, heads, unroll=2)
    def _(h):
        total = tot_ref[h]
        att = att_ref[:, hs(h)] / total
        att_ref[:, hs(h)] = att
        lse_ref[h] = top_ref[h] + jnp.log2(total)
        del_ref[h] = jnp.sum(att * g_ref[:, hs(h)].astype(jnp.float32), axis=1, keepdims=True)

    lane = lax.broadcasted_iota(jnp.int32, (rows, HD), 1)
    packed = jnp.zeros((rows, HD), jnp.float32)
    for h in range(heads):
        packed = jnp.where(lane == h, lse_ref[h], packed)
        packed = jnp.where(lane == heads + h, del_ref[h], packed)
    ld_own[...] = jnp.transpose(packed)[: 2 * heads]

    for d in distances:
        @pl.when(has_before(d))
        def _(d=d):
            ld_copy(d).start()

    def column(h, q, g, lse, delta, keys, values, mask):
        s = dot_nt(keys, q) * SCALE2
        if mask is not None:
            s = jnp.where(mask, s, NEG_FILL)
        p = jnp.exp2(s - lse)
        dp = dot_nt(values, g)
        ds = (p * (dp - delta)).astype(jnp.bfloat16)
        return dot_nn(ds, q), dot_nn(p.astype(jnp.bfloat16), g)

    @pl.when(me >= first)
    def _():
        @pl.loop(0, heads, unroll=2)
        def _(h):
            dk, dv = column(
                h, q_ref[:, hs(h)], g_ref[:, hs(h)],
                ld_own[pl.ds(h, 1)], ld_own[pl.ds(heads + h, 1)],
                pr_buf[0, :, hs(h)], pr_buf[1, :, hs(h)], None,
            )
            pg_out[0, :, hs(h)] = dk.astype(jnp.bfloat16)
            pg_out[1, :, hs(h)] = dv.astype(jnp.bfloat16)

        pg_copy().start()

    def row_backward(h, s, keys, values):
        p = jnp.exp2(s - lse_ref[h])
        dp = dot_nt(g_ref[:, hs(h)], values)
        ds = (p * (dp - del_ref[h])).astype(jnp.bfloat16)
        return dot_nn(ds, keys) * SCALE

    own_cols = (col <= row) & (me * rows + col >= doc_start(me * rows + row))

    @pl.loop(0, heads, unroll=2)
    def _(h):
        dq_ref[:, hs(h)] = row_backward(h, s_buf[0, h], k_ref[:, hs(h)], v_ref[:, hs(h)])
        dk, dv = column(
            h, q_ref[:, hs(h)], g_ref[:, hs(h)],
            ld_own[pl.ds(h, 1)], ld_own[pl.ds(heads + h, 1)],
            k_ref[:, hs(h)], v_ref[:, hs(h)], own_cols,
        )
        dk_ref[:, hs(h)] = dk
        dv_ref[:, hs(h)] = dv

    @pl.when(me >= first)
    def _():
        @pl.loop(0, heads, unroll=2)
        def _(h):
            dq_ref[:, hs(h)] += row_backward(
                h, sp_buf[h], pr_buf[0, :, hs(h)], pr_buf[1, :, hs(h)]
            )

    for d in distances:
        @pl.when(has_before(d))
        def _(d=d):
            @pl.loop(0, heads, unroll=2)
            def _(h):
                dq_ref[:, hs(h)] += row_backward(
                    h, s_buf[d, h], kv_buf[d - 1, 0, :, hs(h)], kv_buf[d - 1, 1, :, hs(h)]
                )

    for d in distances:
        @pl.when(has_after(d))
        def _(d=d):
            for w, c in parts:
                qd_copy(d, w, c).wait_recv()
            ld_copy(d).wait_recv()
            mask = me * rows + col >= doc_start((me + d) * rows + row)

            @pl.loop(0, heads, unroll=2)
            def _(h):
                dk, dv = column(
                    h, qd_buf[d - 1, 0, :, hs(h)], qd_buf[d - 1, 1, :, hs(h)],
                    ld_buf[d - 1, pl.ds(h, 1)], ld_buf[d - 1, pl.ds(heads + h, 1)],
                    k_ref[:, hs(h)], v_ref[:, hs(h)], mask,
                )
                dk_ref[:, hs(h)] += dk
                dv_ref[:, hs(h)] += dv

    @pl.when(me == 0)
    def _():
        @pl.loop(0, later)
        def _(i):
            remote(pg_out, pg_buf.at[i], pg_ss, pg_rs.at[i], 0).wait_recv()
            dk_ref[pl.ds(0, PROMPT)] += pg_buf[i, 0].astype(jnp.float32)
            dv_ref[pl.ds(0, PROMPT)] += pg_buf[i, 1].astype(jnp.float32)

    dk_ref[...] = dk_ref[...] * SCALE

    for d in distances:
        @pl.when(has_after(d))
        def _(d=d):
            for w, c in parts:
                kv_copy(d, w, c).wait_send()

        @pl.when(has_before(d))
        def _(d=d):
            for w, c in parts:
                qd_copy(d, w, c).wait_send()
            ld_copy(d).wait_send()

    @pl.when(me == first)
    def _():
        for w, c in parts:
            kv_relayed(w, c).wait_send()
            qd_relayed(w, c).wait_send()

    @pl.when((me >= first - 2) & (me + 2 < n))
    def _():
        for w in (0, 1):
            pr_copy(pr_buf.at[w], w).wait_send()

    @pl.when(me >= first)
    def _():
        pg_copy().wait_send()


def attention(far, queries, keys, values, out_grad, doc_lengths):
    rows, width = queries.shape
    heads = width // HD
    n = lax.axis_size("ctx")
    first = DOC_MOST // rows
    later = n - first
    reach = max(far, first - 1)
    cuts = rows // PROMPT
    bf, f32 = jnp.bfloat16, jnp.float32
    vmem = pl.BlockSpec(memory_space=pltpu.VMEM)
    hbm = pl.BlockSpec(memory_space=pltpu.HBM)
    dma = pltpu.SemaphoreType.DMA
    tile = rows * rows * heads
    out = jax.ShapeDtypeStruct((rows, width), f32)
    return pl.pallas_call(
        functools.partial(kernel, n, first, far),
        out_shape=[out] * 4,
        in_specs=[pl.BlockSpec(memory_space=pltpu.SMEM)] + [hbm] * 4,
        out_specs=[vmem] * 4,
        scratch_shapes=[pltpu.VMEM((rows, width), bf)] * 4
        + [
            pltpu.VMEM((reach, 2, rows, width), bf),
            pltpu.VMEM((reach, 2, rows, width), bf),
            pltpu.VMEM((2, 2, rows, width), bf),
            pltpu.VMEM((2, PROMPT, width), bf),
            pltpu.VMEM((2, PROMPT, width), bf),
            pltpu.VMEM((later, 2, PROMPT, width), bf),
            pltpu.VMEM((2 * heads, rows), f32),
            pltpu.VMEM((reach, 2 * heads, rows), f32),
            pltpu.VMEM((reach + 1, heads, rows, rows), f32),
            pltpu.VMEM((heads, rows, PROMPT), f32),
            pltpu.VMEM((heads, rows, 1), f32),
            pltpu.VMEM((heads, rows, 1), f32),
            pltpu.VMEM((heads, rows, 1), f32),
            pltpu.VMEM((heads, rows, 1), f32),
            dma((reach, 2, cuts)), dma((reach, 2, cuts)),
            dma((reach, 2, cuts)), dma((reach, 2, cuts)),
            dma((reach,)), dma((reach,)),
            dma((2,)), dma((2,)),
            dma(()), dma((later,)),
            dma((2, 2, cuts)), dma((2, 2, cuts)), dma((4,)),
        ],
        compiler_params=pltpu.CompilerParams(
            collective_id=far, has_side_effects=True, vmem_limit_bytes=48 * 2**20
        ),
        cost_estimate=pl.CostEstimate(
            flops=2 * 8 * 4 * tile * HD, bytes_accessed=12 * rows * width, transcendentals=8 * tile
        ),
    )(doc_lengths, queries, keys, values, out_grad)


def on_device(queries, keys, values, out_grad, doc_lengths):
    rows = queries.shape[0]
    docs = doc_lengths.shape[0]
    order = jnp.arange(docs)
    ends = jnp.sum(jnp.where(order[:, None] <= order[None, :], doc_lengths[:, None], 0), axis=0)
    span = (ends - 1) // rows - (ends - doc_lengths) // rows
    far = jnp.any((span > 1) & (order > 0))
    return lax.cond(
        far,
        functools.partial(attention, REACH),
        functools.partial(attention, 1),
        queries, keys, values, out_grad, doc_lengths,
    )


def solution(mesh):
    block = P("ctx", "head")
    return jax.shard_map(
        on_device, mesh=mesh, in_specs=(block,) * 4 + (P(),), out_specs=(block,) * 4, check_vma=False
    )
```

```python
import functools
import math

import jax
import jax.numpy as jnp
from jax import lax
from jax.experimental import pallas as pl
from jax.experimental.pallas import tpu as pltpu
from jax.sharding import PartitionSpec as P

HD = 128
PROMPT = 64
DOC_MOST = 768
REACH = 3
NEG_FILL = -1e30
SCALE = 1.0 / math.sqrt(HD)
SCALE2 = SCALE * math.log2(math.e)
MESH = pl.DeviceIdType.MESH


def remote(src, dst, send_sem, recv_sem, target):
    return pltpu.make_async_remote_copy(
        src_ref=src,
        dst_ref=dst,
        send_sem=send_sem,
        recv_sem=recv_sem,
        device_id={"ctx": target},
        device_id_type=MESH,
    )


def dot_nt(a, b):
    return lax.dot_general(a, b, (((1,), (1,)), ((), ())), preferred_element_type=jnp.float32)


def dot_nn(a, b):
    return jnp.dot(a, b, preferred_element_type=jnp.float32)


def dot_tn(a, b):
    return lax.dot_general(a, b, (((0,), (0,)), ((), ())), preferred_element_type=jnp.float32)


def kernel(
    n, first, far, len_ref, q_hbm, k_hbm, v_hbm, g_hbm,
    att_ref, dq_ref, dk_ref, dv_ref,
    q_ref, k_ref, v_ref, g_ref, kv_buf, qd_buf, rl_buf, pr_buf, pg_out, pg_buf, ld_own, ld_buf,
    s_buf, sp_buf, top_ref, tot_ref, out_t, dq_t,
    kv_ss, kv_rs, qd_ss, qd_rs, ld_ss, ld_rs, pr_ss, pr_rs, pg_ss, pg_rs, rl_ss, rl_rs, in_sem,
):
    rows, width = q_ref.shape
    heads = width // HD
    docs = len_ref.shape[0]
    me = lax.axis_index("ctx")
    later = n - first
    reach = max(far, first - 1)
    chunks = [pl.ds(c * PROMPT, PROMPT) for c in range(rows // PROMPT)]

    def has_before(d):
        near = (me >= d) & (me < first)
        return near | (me >= first + d) if d <= far else near

    def has_after(d):
        near = me + d < first
        return near | ((me >= first) & (me + d < n)) if d <= far else near

    own_copies = [
        pltpu.make_async_copy(src, dst, in_sem.at[i])
        for i, (src, dst) in enumerate(
            ((q_hbm, q_ref), (k_hbm, k_ref), (v_hbm, v_ref), (g_hbm, g_ref))
        )
    ]
    for copy in own_copies:
        copy.start()

    barrier = pltpu.get_barrier_semaphore()
    for s in range(1, n):
        pl.semaphore_signal(
            barrier, inc=1, device_id={"ctx": lax.rem(me + s, n)}, device_id_type=MESH
        )
    pl.semaphore_wait(barrier, n - 1)

    def kv_copy(d, w, c):
        src = (k_hbm, v_hbm)[w]
        return remote(
            src.at[chunks[c]], kv_buf.at[d - 1, w, chunks[c]],
            kv_ss.at[d - 1, w, c], kv_rs.at[d - 1, w, c], lax.rem(me + d, n),
        )

    def qd_copy(d, w, c):
        src = (q_hbm, g_hbm)[w]
        return remote(
            src.at[chunks[c]], qd_buf.at[d - 1, w, chunks[c]],
            qd_ss.at[d - 1, w, c], qd_rs.at[d - 1, w, c], lax.rem(me + n - d, n),
        )

    def qd_to_relay(w, c):
        src = (q_hbm, g_hbm)[w]
        return remote(
            src.at[chunks[c]], rl_buf.at[w, chunks[c]], qd_ss.at[0, w, c], rl_rs.at[w, c], first
        )

    def qd_relayed(w, c):
        return remote(
            rl_buf.at[w, chunks[c]], qd_buf.at[0, w, chunks[c]],
            rl_ss.at[w, c], qd_rs.at[0, w, c], first - 2,
        )

    parts = [(w, c) for c in range(len(chunks)) for w in (0, 1)]

    def ld_copy(d):
        return remote(
            ld_own, ld_buf.at[d - 1], ld_ss.at[d - 1], ld_rs.at[d - 1], lax.rem(me + n - d, n)
        )

    def pr_copy(src, w):
        return remote(src, pr_buf.at[w], pr_ss.at[w], pr_rs.at[w], lax.rem(me + 2, n))

    def pg_copy():
        slot = lax.rem(me + n - first, n)
        return remote(pg_out, pg_buf.at[slot], pg_ss, pg_rs.at[slot], 0)

    distances = range(1, reach + 1)

    for c in range(len(chunks)):
        for d in distances:
            @pl.when(has_after(d))
            def _(d=d, c=c):
                for w in (0, 1):
                    kv_copy(d, w, c).start()

    @pl.when(me == first - 1)
    def _():
        for w, c in parts:
            qd_to_relay(w, c).start()
            for d in range(2, first):
                qd_copy(d, w, c).start()

    for holder in (first - 2, first - 1):
        @pl.when(me == holder)
        def _(holder=holder):
            for w in (0, 1):
                kv_copy(holder, w, 0).wait_recv()
                pr_copy(kv_buf.at[holder - 1, w, pl.ds(0, PROMPT)], w).start()

    def pass_prompt():
        for w in (0, 1):
            pr_copy(pr_buf.at[w], w).wait_recv()

            @pl.when(me + 2 < n)
            def _(w=w):
                pr_copy(pr_buf.at[w], w).start()

    @pl.when(me == first)
    def _():
        def relay(some):
            for w, c in some:
                remote(
                    rl_buf.at[w, chunks[c]], rl_buf.at[w, chunks[c]],
                    rl_ss.at[w, c], rl_rs.at[w, c], first - 1,
                ).wait_recv()
                qd_relayed(w, c).start()

        relay(parts[: len(parts) // 2])
        pass_prompt()
        relay(parts[len(parts) // 2 :])

    for copy in own_copies:
        copy.wait()

    def doc_start(pos):
        start = jnp.zeros_like(pos)
        end = jnp.int32(0)
        for i in range(docs):
            end = end + len_ref[i]
            start = jnp.where(pos >= end, end, start)
        return start

    u_pos = me * rows + lax.broadcasted_iota(jnp.int32, (rows, 1), 0)
    t_pos = me * rows + lax.broadcasted_iota(jnp.int32, (1, rows), 1)
    t_start = doc_start(t_pos)

    def hs(h):
        return pl.ds(pl.multiple_of(h * HD, HD), HD)

    def forward(h, keys, values, mask):
        s = dot_nt(keys, q_ref[:, hs(h)]) * SCALE2
        if mask is not None:
            s = jnp.where(mask, s, NEG_FILL)
        top = top_ref[pl.ds(h, 1)]
        fresh = jnp.maximum(top, jnp.max(s, axis=0, keepdims=True))
        fade = jnp.exp2(top - fresh)
        p = jnp.exp2(s - fresh)
        top_ref[pl.ds(h, 1)] = fresh
        tot_ref[pl.ds(h, 1)] = tot_ref[pl.ds(h, 1)] * fade + jnp.sum(p, axis=0, keepdims=True)
        out_t[h] = out_t[h] * fade + dot_tn(values, p.astype(jnp.bfloat16))
        return s

    own_mask = (u_pos <= t_pos) & (u_pos >= t_start)

    @pl.loop(0, heads, unroll=2)
    def _(h):
        s = dot_nt(k_ref[:, hs(h)], q_ref[:, hs(h)]) * SCALE2
        s = jnp.where(own_mask, s, NEG_FILL)
        top = jnp.max(s, axis=0, keepdims=True)
        p = jnp.exp2(s - top)
        s_buf[0, h] = s
        top_ref[pl.ds(h, 1)] = top
        tot_ref[pl.ds(h, 1)] = jnp.sum(p, axis=0, keepdims=True)
        out_t[h] = dot_tn(v_ref[:, hs(h)], p.astype(jnp.bfloat16))

    @pl.when(me > first)
    def _():
        pass_prompt()

    @pl.when(me >= first)
    def _():
        @pl.loop(0, heads, unroll=2)
        def _(h):
            sp_buf[h] = forward(h, pr_buf[0, :, hs(h)], pr_buf[1, :, hs(h)], None)

    for d in distances:
        @pl.when(has_before(d))
        def _(d=d):
            for w, c in parts:
                if c == 0 and d in (first - 2, first - 1):
                    @pl.when(me != d)
                    def _(w=w):
                        kv_copy(d, w, 0).wait_recv()
                else:
                    kv_copy(d, w, c).wait_recv()
            if d == 1:
                for e in distances:
                    @pl.when(has_before(e) & (me != first - 1))
                    def _(e=e):
                        for w, c in parts:
                            qd_copy(e, w, c).start()
            mask = u_pos - d * rows >= t_start

            @pl.loop(0, heads, unroll=2)
            def _(h):
                s_buf[d, h] = forward(
                    h, kv_buf[d - 1, 0, :, hs(h)], kv_buf[d - 1, 1, :, hs(h)], mask
                )

    @pl.loop(0, heads, unroll=2)
    def _(h):
        total = tot_ref[pl.ds(h, 1)]
        out = out_t[h] / total
        att_ref[:, hs(h)] = jnp.transpose(out)
        grad = jnp.transpose(g_ref[:, hs(h)].astype(jnp.float32))
        ld_own[pl.ds(h, 1)] = top_ref[pl.ds(h, 1)] + jnp.log2(total)
        ld_own[pl.ds(heads + h, 1)] = jnp.sum(out * grad, axis=0, keepdims=True)

    for d in distances:
        @pl.when(has_before(d))
        def _(d=d):
            ld_copy(d).start()

    def backward(s, g, lse, delta, values):
        p = jnp.exp2(s - lse)
        dp = dot_nt(values, g)
        return p.astype(jnp.bfloat16), (p * (dp - delta)).astype(jnp.bfloat16)

    def own_backward(h, s, values):
        return backward(
            s, g_ref[:, hs(h)], ld_own[pl.ds(h, 1)], ld_own[pl.ds(heads + h, 1)], values
        )

    @pl.when(me >= first)
    def _():
        @pl.loop(0, heads, unroll=2)
        def _(h):
            p, ds = own_backward(h, sp_buf[h], pr_buf[1, :, hs(h)])
            pg_out[0, :, hs(h)] = dot_nn(ds, q_ref[:, hs(h)]).astype(jnp.bfloat16)
            pg_out[1, :, hs(h)] = dot_nn(p, g_ref[:, hs(h)]).astype(jnp.bfloat16)
            dq_t[h] = dot_tn(pr_buf[0, :, hs(h)], ds)

        pg_copy().start()

    @pl.when(me < first)
    def _():
        dq_t[...] = jnp.zeros_like(dq_t)

    @pl.loop(0, heads, unroll=2)
    def _(h):
        p, ds = own_backward(h, s_buf[0, h], v_ref[:, hs(h)])
        dk_ref[:, hs(h)] = dot_nn(ds, q_ref[:, hs(h)])
        dv_ref[:, hs(h)] = dot_nn(p, g_ref[:, hs(h)])
        dq_t[h] += dot_tn(k_ref[:, hs(h)], ds)

    for d in distances:
        @pl.when(has_before(d))
        def _(d=d):
            @pl.loop(0, heads, unroll=2)
            def _(h):
                p, ds = own_backward(h, s_buf[d, h], kv_buf[d - 1, 1, :, hs(h)])
                dq_t[h] += dot_tn(kv_buf[d - 1, 0, :, hs(h)], ds)

    @pl.loop(0, heads, unroll=2)
    def _(h):
        dq_ref[:, hs(h)] = jnp.transpose(dq_t[h] * SCALE)

    for d in distances:
        @pl.when(has_after(d))
        def _(d=d):
            for w, c in parts:
                qd_copy(d, w, c).wait_recv()
            ld_copy(d).wait_recv()
            mask = u_pos >= doc_start(t_pos + d * rows)

            @pl.loop(0, heads, unroll=2)
            def _(h):
                q = qd_buf[d - 1, 0, :, hs(h)]
                g = qd_buf[d - 1, 1, :, hs(h)]
                s = jnp.where(mask, dot_nt(k_ref[:, hs(h)], q) * SCALE2, NEG_FILL)
                p, ds = backward(
                    s, g, ld_buf[d - 1, pl.ds(h, 1)], ld_buf[d - 1, pl.ds(heads + h, 1)],
                    v_ref[:, hs(h)],
                )
                dk_ref[:, hs(h)] += dot_nn(ds, q)
                dv_ref[:, hs(h)] += dot_nn(p, g)

    @pl.when(me == 0)
    def _():
        @pl.loop(0, later)
        def _(i):
            remote(pg_out, pg_buf.at[i], pg_ss, pg_rs.at[i], 0).wait_recv()
            dk_ref[pl.ds(0, PROMPT)] += pg_buf[i, 0].astype(jnp.float32)
            dv_ref[pl.ds(0, PROMPT)] += pg_buf[i, 1].astype(jnp.float32)

    dk_ref[...] = dk_ref[...] * SCALE

    for d in distances:
        @pl.when(has_after(d))
        def _(d=d):
            for w, c in parts:
                kv_copy(d, w, c).wait_send()

        @pl.when(has_before(d))
        def _(d=d):
            for w, c in parts:
                qd_copy(d, w, c).wait_send()
            ld_copy(d).wait_send()

    @pl.when(me == first)
    def _():
        for w, c in parts:
            qd_relayed(w, c).wait_send()

    @pl.when((me >= first - 2) & (me + 2 < n))
    def _():
        for w in (0, 1):
            pr_copy(pr_buf.at[w], w).wait_send()

    @pl.when(me >= first)
    def _():
        pg_copy().wait_send()


def attention(far, queries, keys, values, out_grad, doc_lengths):
    rows, width = queries.shape
    heads = width // HD
    n = lax.axis_size("ctx")
    first = DOC_MOST // rows
    later = n - first
    reach = max(far, first - 1)
    cuts = rows // PROMPT
    bf, f32 = jnp.bfloat16, jnp.float32
    vmem = pl.BlockSpec(memory_space=pltpu.VMEM)
    hbm = pl.BlockSpec(memory_space=pltpu.HBM)
    dma = pltpu.SemaphoreType.DMA
    tile = rows * rows * heads
    out = jax.ShapeDtypeStruct((rows, width), f32)
    return pl.pallas_call(
        functools.partial(kernel, n, first, far),
        out_shape=[out] * 4,
        in_specs=[pl.BlockSpec(memory_space=pltpu.SMEM)] + [hbm] * 4,
        out_specs=[vmem] * 4,
        scratch_shapes=[pltpu.VMEM((rows, width), bf)] * 4
        + [
            pltpu.VMEM((reach, 2, rows, width), bf),
            pltpu.VMEM((reach, 2, rows, width), bf),
            pltpu.VMEM((2, rows, width), bf),
            pltpu.VMEM((2, PROMPT, width), bf),
            pltpu.VMEM((2, PROMPT, width), bf),
            pltpu.VMEM((later, 2, PROMPT, width), bf),
            pltpu.VMEM((2 * heads, rows), f32),
            pltpu.VMEM((reach, 2 * heads, rows), f32),
            pltpu.VMEM((reach + 1, heads, rows, rows), f32),
            pltpu.VMEM((heads, PROMPT, rows), f32),
            pltpu.VMEM((heads, rows), f32),
            pltpu.VMEM((heads, rows), f32),
            pltpu.VMEM((heads, HD, rows), f32),
            pltpu.VMEM((heads, HD, rows), f32),
            dma((reach, 2, cuts)), dma((reach, 2, cuts)),
            dma((reach, 2, cuts)), dma((reach, 2, cuts)),
            dma((reach,)), dma((reach,)),
            dma((2,)), dma((2,)),
            dma(()), dma((later,)),
            dma((2, cuts)), dma((2, cuts)), dma((4,)),
        ],
        compiler_params=pltpu.CompilerParams(
            collective_id=far, has_side_effects=True, vmem_limit_bytes=48 * 2**20
        ),
        cost_estimate=pl.CostEstimate(
            flops=2 * 8 * 4 * tile * HD, bytes_accessed=12 * rows * width, transcendentals=8 * tile
        ),
    )(doc_lengths, queries, keys, values, out_grad)


def on_device(queries, keys, values, out_grad, doc_lengths):
    rows = queries.shape[0]
    docs = doc_lengths.shape[0]
    order = jnp.arange(docs)
    ends = jnp.sum(jnp.where(order[:, None] <= order[None, :], doc_lengths[:, None], 0), axis=0)
    span = (ends - 1) // rows - (ends - doc_lengths) // rows
    far = jnp.any((span > 1) & (order > 0))
    return lax.cond(
        far,
        functools.partial(attention, REACH),
        functools.partial(attention, 1),
        queries, keys, values, out_grad, doc_lengths,
    )


def solution(mesh):
    block = P("ctx", "head")
    return jax.shard_map(
        on_device, mesh=mesh, in_specs=(block,) * 4 + (P(),), out_specs=(block,) * 4, check_vma=False
    )
```

```python
import functools
import math

import jax
import jax.numpy as jnp
from jax import lax
from jax.experimental import pallas as pl
from jax.experimental.pallas import tpu as pltpu
from jax.sharding import PartitionSpec as P

HD = 128
PROMPT = 64
DOC_MOST = 768
REACH = 3
NEG_FILL = -1e30
SCALE = 1.0 / math.sqrt(HD)
SCALE2 = SCALE * math.log2(math.e)
MESH = pl.DeviceIdType.MESH


def remote(src, dst, send_sem, recv_sem, target):
    return pltpu.make_async_remote_copy(
        src_ref=src,
        dst_ref=dst,
        send_sem=send_sem,
        recv_sem=recv_sem,
        device_id={"ctx": target},
        device_id_type=MESH,
    )


def dot_nt(a, b):
    return lax.dot_general(a, b, (((1,), (1,)), ((), ())), preferred_element_type=jnp.float32)


def dot_nn(a, b):
    return jnp.dot(a, b, preferred_element_type=jnp.float32)


def dot_tn(a, b):
    return lax.dot_general(a, b, (((0,), (0,)), ((), ())), preferred_element_type=jnp.float32)


def kernel(
    n, first, far, len_ref, q_hbm, k_hbm, v_hbm, g_hbm,
    att_ref, dq_ref, dk_ref, dv_ref,
    q_ref, k_ref, v_ref, g_ref, kv_buf, qd_buf, rl_buf, pr_buf, pg_out, pg_buf, ld_own, ld_buf,
    s_buf, sp_buf, top_ref, tot_ref, out_t, dq_t,
    kv_ss, kv_rs, qd_ss, qd_rs, ld_ss, ld_rs, pr_ss, pr_rs, pg_ss, pg_rs, rl_ss, rl_rs, in_sem,
):
    rows, width = q_ref.shape
    heads = width // HD
    docs = len_ref.shape[0]
    me = lax.axis_index("ctx")
    later = n - first
    reach = max(far, first - 1)
    chunks = [pl.ds(c * PROMPT, PROMPT) for c in range(rows // PROMPT)]

    def has_before(d):
        near = (me >= d) & (me < first)
        return near | (me >= first + d) if d <= far else near

    def has_after(d):
        near = me + d < first
        return near | ((me >= first) & (me + d < n)) if d <= far else near

    own_copies = [
        pltpu.make_async_copy(src, dst, in_sem.at[i])
        for i, (src, dst) in enumerate(
            ((q_hbm, q_ref), (k_hbm, k_ref), (v_hbm, v_ref), (g_hbm, g_ref))
        )
    ]
    for copy in own_copies:
        copy.start()

    barrier = pltpu.get_barrier_semaphore()
    for s in range(1, n):
        pl.semaphore_signal(
            barrier, inc=1, device_id={"ctx": lax.rem(me + s, n)}, device_id_type=MESH
        )
    pl.semaphore_wait(barrier, n - 1)

    def kv_copy(d, w, c):
        src = (k_hbm, v_hbm)[w]
        return remote(
            src.at[chunks[c]], kv_buf.at[d - 1, w, chunks[c]],
            kv_ss.at[d - 1, w, c], kv_rs.at[d - 1, w, c], lax.rem(me + d, n),
        )

    def qd_copy(d, w, c):
        src = (q_hbm, g_hbm)[w]
        return remote(
            src.at[chunks[c]], qd_buf.at[d - 1, w, chunks[c]],
            qd_ss.at[d - 1, w, c], qd_rs.at[d - 1, w, c], lax.rem(me + n - d, n),
        )

    def qd_to_relay(w, c):
        src = (q_hbm, g_hbm)[w]
        return remote(
            src.at[chunks[c]], rl_buf.at[w, chunks[c]], qd_ss.at[0, w, c], rl_rs.at[w, c], first
        )

    def qd_relayed(w, c):
        return remote(
            rl_buf.at[w, chunks[c]], qd_buf.at[0, w, chunks[c]],
            rl_ss.at[w, c], qd_rs.at[0, w, c], first - 2,
        )

    parts = [(w, c) for c in range(len(chunks)) for w in (0, 1)]

    def ld_copy(d):
        return remote(
            ld_own, ld_buf.at[d - 1], ld_ss.at[d - 1], ld_rs.at[d - 1], lax.rem(me + n - d, n)
        )

    def pr_source(t):
        return (t + 1 - first % 2) % 2 if t < first + 4 else t - 4

    def pr_slot(t):
        return 0 if t >= first + 4 else (t - first) // 2

    def pr_copy(t, w):
        source = pr_source(t)
        if source == 0:
            src = (k_hbm, v_hbm)[w].at[chunks[0]]
        elif source == 1:
            src = kv_buf.at[0, w, chunks[0]]
        else:
            src = pr_buf.at[w]
        slot = pr_slot(t)
        return remote(src, pr_buf.at[w], pr_ss.at[slot, w], pr_rs.at[w], t)

    def pass_prompt(w):
        for t in range(first, n):
            @pl.when(me == pr_source(t))
            def _(t=t):
                pr_copy(t, w).start()

    def take_prompt():
        for w in (0, 1):
            remote(pr_buf.at[w], pr_buf.at[w], pr_ss.at[0, w], pr_rs.at[w], first).wait_recv()
            pass_prompt(w)

    def pg_copy():
        slot = lax.rem(me + n - first, n)
        return remote(pg_out, pg_buf.at[slot], pg_ss, pg_rs.at[slot], 0)

    distances = range(1, reach + 1)
    for c in range(len(chunks)):
        for d in distances:
            @pl.when(has_after(d))
            def _(d=d, c=c):
                for w in (0, 1):
                    kv_copy(d, w, c).start()
        if c == 0:
            @pl.when(me == 0)
            def _():
                for w in (0, 1):
                    pass_prompt(w)

    direct, by_relay = parts[: len(parts) // 2], parts[len(parts) // 2 :]

    @pl.when(me == first - 1)
    def _():
        for w, c in by_relay:
            qd_to_relay(w, c).start()
        for w, c in direct:
            qd_copy(1, w, c).start()

    for d in distances:
        others = (me != first - 1) if d == 1 else (me >= 0)

        @pl.when(has_before(d) & others)
        def _(d=d):
            for w, c in parts:
                qd_copy(d, w, c).start()

    @pl.when(me == 1)
    def _():
        for w in (0, 1):
            kv_copy(1, w, 0).wait_recv()
            pass_prompt(w)

    @pl.when(me == first)
    def _():
        def relay(some):
            for w, c in some:
                remote(
                    rl_buf.at[w, chunks[c]], rl_buf.at[w, chunks[c]],
                    rl_ss.at[w, c], rl_rs.at[w, c], first - 1,
                ).wait_recv()
                qd_relayed(w, c).start()

        relay(by_relay[:2])
        take_prompt()
        relay(by_relay[2:])

    for copy in own_copies:
        copy.wait()

    def doc_start(pos):
        start = jnp.zeros_like(pos)
        end = jnp.int32(0)
        for i in range(docs):
            end = end + len_ref[i]
            start = jnp.where(pos >= end, end, start)
        return start

    u_pos = me * rows + lax.broadcasted_iota(jnp.int32, (rows, 1), 0)
    t_pos = me * rows + lax.broadcasted_iota(jnp.int32, (1, rows), 1)
    t_start = doc_start(t_pos)

    def hs(h):
        return pl.ds(pl.multiple_of(h * HD, HD), HD)

    def forward(h, keys, values, mask):
        s = dot_nt(keys, q_ref[:, hs(h)]) * SCALE2
        if mask is not None:
            s = jnp.where(mask, s, NEG_FILL)
        top = top_ref[pl.ds(h, 1)]
        fresh = jnp.maximum(top, jnp.max(s, axis=0, keepdims=True))
        fade = jnp.exp2(top - fresh)
        p = jnp.exp2(s - fresh)
        top_ref[pl.ds(h, 1)] = fresh
        tot_ref[pl.ds(h, 1)] = tot_ref[pl.ds(h, 1)] * fade + jnp.sum(p, axis=0, keepdims=True)
        out_t[h] = out_t[h] * fade + dot_tn(values, p.astype(jnp.bfloat16))
        return s

    own_mask = (u_pos <= t_pos) & (u_pos >= t_start)

    @pl.loop(0, heads, unroll=2)
    def _(h):
        s = dot_nt(k_ref[:, hs(h)], q_ref[:, hs(h)]) * SCALE2
        s = jnp.where(own_mask, s, NEG_FILL)
        top = jnp.max(s, axis=0, keepdims=True)
        p = jnp.exp2(s - top)
        s_buf[0, h] = s
        top_ref[pl.ds(h, 1)] = top
        tot_ref[pl.ds(h, 1)] = jnp.sum(p, axis=0, keepdims=True)
        out_t[h] = dot_tn(v_ref[:, hs(h)], p.astype(jnp.bfloat16))

    @pl.when(me > first)
    def _():
        take_prompt()

    @pl.when(me >= first)
    def _():
        @pl.loop(0, heads, unroll=2)
        def _(h):
            sp_buf[h] = forward(h, pr_buf[0, :, hs(h)], pr_buf[1, :, hs(h)], None)

    for d in distances:
        @pl.when(has_before(d))
        def _(d=d):
            for w, c in parts:
                if c == 0 and d == 1:
                    @pl.when(me != 1)
                    def _(w=w):
                        kv_copy(1, w, 0).wait_recv()
                else:
                    kv_copy(d, w, c).wait_recv()
            mask = u_pos - d * rows >= t_start

            @pl.loop(0, heads, unroll=2)
            def _(h):
                s_buf[d, h] = forward(
                    h, kv_buf[d - 1, 0, :, hs(h)], kv_buf[d - 1, 1, :, hs(h)], mask
                )

    @pl.loop(0, heads, unroll=2)
    def _(h):
        total = tot_ref[pl.ds(h, 1)]
        out = out_t[h] / total
        att_ref[:, hs(h)] = jnp.transpose(out)
        grad = jnp.transpose(g_ref[:, hs(h)].astype(jnp.float32))
        ld_own[pl.ds(h, 1)] = top_ref[pl.ds(h, 1)] + jnp.log2(total)
        ld_own[pl.ds(heads + h, 1)] = jnp.sum(out * grad, axis=0, keepdims=True)

    for d in distances:
        @pl.when(has_before(d))
        def _(d=d):
            ld_copy(d).start()

    def backward(s, g, lse, delta, values):
        p = jnp.exp2(s - lse)
        dp = dot_nt(values, g)
        return p.astype(jnp.bfloat16), (p * (dp - delta)).astype(jnp.bfloat16)

    def own_backward(h, s, values):
        return backward(
            s, g_ref[:, hs(h)], ld_own[pl.ds(h, 1)], ld_own[pl.ds(heads + h, 1)], values
        )

    @pl.when(me >= first)
    def _():
        @pl.loop(0, heads, unroll=2)
        def _(h):
            p, ds = own_backward(h, sp_buf[h], pr_buf[1, :, hs(h)])
            pg_out[0, :, hs(h)] = dot_nn(ds, q_ref[:, hs(h)]).astype(jnp.bfloat16)
            pg_out[1, :, hs(h)] = dot_nn(p, g_ref[:, hs(h)]).astype(jnp.bfloat16)
            dq_t[h] = dot_tn(pr_buf[0, :, hs(h)], ds)

        pg_copy().start()

    @pl.when(me < first)
    def _():
        dq_t[...] = jnp.zeros_like(dq_t)

    @pl.loop(0, heads, unroll=2)
    def _(h):
        p, ds = own_backward(h, s_buf[0, h], v_ref[:, hs(h)])
        dk_ref[:, hs(h)] = dot_nn(ds, q_ref[:, hs(h)])
        dv_ref[:, hs(h)] = dot_nn(p, g_ref[:, hs(h)])
        dq_t[h] += dot_tn(k_ref[:, hs(h)], ds)

    for d in distances:
        @pl.when(has_before(d))
        def _(d=d):
            @pl.loop(0, heads, unroll=2)
            def _(h):
                p, ds = own_backward(h, s_buf[d, h], kv_buf[d - 1, 1, :, hs(h)])
                dq_t[h] += dot_tn(kv_buf[d - 1, 0, :, hs(h)], ds)

    @pl.loop(0, heads, unroll=2)
    def _(h):
        dq_ref[:, hs(h)] = jnp.transpose(dq_t[h] * SCALE)

    for d in distances:
        @pl.when(has_after(d))
        def _(d=d):
            for w, c in parts:
                qd_copy(d, w, c).wait_recv()
            ld_copy(d).wait_recv()
            mask = u_pos >= doc_start(t_pos + d * rows)

            @pl.loop(0, heads, unroll=2)
            def _(h):
                q = qd_buf[d - 1, 0, :, hs(h)]
                g = qd_buf[d - 1, 1, :, hs(h)]
                s = jnp.where(mask, dot_nt(k_ref[:, hs(h)], q) * SCALE2, NEG_FILL)
                p, ds = backward(
                    s, g, ld_buf[d - 1, pl.ds(h, 1)], ld_buf[d - 1, pl.ds(heads + h, 1)],
                    v_ref[:, hs(h)],
                )
                dk_ref[:, hs(h)] += dot_nn(ds, q)
                dv_ref[:, hs(h)] += dot_nn(p, g)

    @pl.when(me == 0)
    def _():
        @pl.loop(0, later)
        def _(i):
            remote(pg_out, pg_buf.at[i], pg_ss, pg_rs.at[i], 0).wait_recv()
            dk_ref[pl.ds(0, PROMPT)] += pg_buf[i, 0].astype(jnp.float32)
            dv_ref[pl.ds(0, PROMPT)] += pg_buf[i, 1].astype(jnp.float32)

    dk_ref[...] = dk_ref[...] * SCALE

    for d in distances:
        @pl.when(has_after(d))
        def _(d=d):
            for w, c in parts:
                kv_copy(d, w, c).wait_send()

        @pl.when(has_before(d))
        def _(d=d):
            for w, c in parts:
                qd_copy(d, w, c).wait_send()
            ld_copy(d).wait_send()

    @pl.when(me == first)
    def _():
        for w, c in by_relay:
            qd_relayed(w, c).wait_send()

    for t in range(first, n):
        @pl.when(me == pr_source(t))
        def _(t=t):
            for w in (0, 1):
                pr_copy(t, w).wait_send()

    @pl.when(me >= first)
    def _():
        pg_copy().wait_send()


def attention(far, queries, keys, values, out_grad, doc_lengths):
    rows, width = queries.shape
    heads = width // HD
    n = lax.axis_size("ctx")
    first = DOC_MOST // rows
    later = n - first
    reach = max(far, first - 1)
    cuts = rows // PROMPT
    bf, f32 = jnp.bfloat16, jnp.float32
    vmem = pl.BlockSpec(memory_space=pltpu.VMEM)
    hbm = pl.BlockSpec(memory_space=pltpu.HBM)
    dma = pltpu.SemaphoreType.DMA
    tile = rows * rows * heads
    out = jax.ShapeDtypeStruct((rows, width), f32)
    return pl.pallas_call(
        functools.partial(kernel, n, first, far),
        out_shape=[out] * 4,
        in_specs=[pl.BlockSpec(memory_space=pltpu.SMEM)] + [hbm] * 4,
        out_specs=[vmem] * 4,
        scratch_shapes=[pltpu.VMEM((rows, width), bf)] * 4
        + [
            pltpu.VMEM((reach, 2, rows, width), bf),
            pltpu.VMEM((reach, 2, rows, width), bf),
            pltpu.VMEM((2, rows, width), bf),
            pltpu.VMEM((2, PROMPT, width), bf),
            pltpu.VMEM((2, PROMPT, width), bf),
            pltpu.VMEM((later, 2, PROMPT, width), bf),
            pltpu.VMEM((2 * heads, rows), f32),
            pltpu.VMEM((reach, 2 * heads, rows), f32),
            pltpu.VMEM((reach + 1, heads, rows, rows), f32),
            pltpu.VMEM((heads, PROMPT, rows), f32),
            pltpu.VMEM((heads, rows), f32),
            pltpu.VMEM((heads, rows), f32),
            pltpu.VMEM((heads, HD, rows), f32),
            pltpu.VMEM((heads, HD, rows), f32),
            dma((reach, 2, cuts)), dma((reach, 2, cuts)),
            dma((reach, 2, cuts)), dma((reach, 2, cuts)),
            dma((reach,)), dma((reach,)),
            dma((2, 2)), dma((2,)),
            dma(()), dma((later,)),
            dma((2, cuts)), dma((2, cuts)), dma((4,)),
        ],
        compiler_params=pltpu.CompilerParams(
            collective_id=far, has_side_effects=True, vmem_limit_bytes=48 * 2**20
        ),
        cost_estimate=pl.CostEstimate(
            flops=2 * 8 * 4 * tile * HD, bytes_accessed=12 * rows * width, transcendentals=8 * tile
        ),
    )(doc_lengths, queries, keys, values, out_grad)


def write_kernel(*refs):
    count = len(refs) // 2
    copies = []
    for i in range(count):
        half = refs[i].shape[0] // 2
        for j in (0, 1):
            part = pl.ds(j * half, half)
            copies.append(
                pltpu.make_async_copy(
                    refs[i].at[part], refs[count + i].at[part], refs[-1].at[i, j]
                )
            )
    for copy in copies:
        copy.start()
    for copy in copies:
        copy.wait()


def written(arrays):
    hbm = pl.BlockSpec(memory_space=pltpu.HBM)
    return pl.pallas_call(
        write_kernel,
        out_shape=[jax.ShapeDtypeStruct(a.shape, a.dtype) for a in arrays],
        in_specs=[pl.BlockSpec(memory_space=pl.ANY)] * len(arrays),
        out_specs=[hbm] * len(arrays),
        scratch_shapes=[pltpu.SemaphoreType.DMA((len(arrays), 2))],
        compiler_params=pltpu.CompilerParams(vmem_limit_bytes=2**20),
    )(*arrays)


def on_device(queries, keys, values, out_grad, doc_lengths):
    rows = queries.shape[0]
    docs = doc_lengths.shape[0]
    order = jnp.arange(docs)
    ends = jnp.sum(jnp.where(order[:, None] <= order[None, :], doc_lengths[:, None], 0), axis=0)
    span = (ends - 1) // rows - (ends - doc_lengths) // rows
    far = jnp.any((span > 1) & (order > 0))
    arrays = lax.cond(
        far,
        functools.partial(attention, REACH),
        functools.partial(attention, 1),
        queries, keys, values, out_grad, doc_lengths,
    )
    return tuple(written(arrays))


def solution(mesh):
    block = P("ctx", "head")
    return jax.shard_map(
        on_device, mesh=mesh, in_specs=(block,) * 4 + (P(),), out_specs=(block,) * 4, check_vma=False
    )
```

```python
import functools
import math

import jax
import jax.numpy as jnp
from jax import lax
from jax.experimental import pallas as pl
from jax.experimental.pallas import tpu as pltpu
from jax.sharding import PartitionSpec as P

HD = 128
PROMPT = 64
DOC_MOST = 768
REACH = 3
NEG_FILL = -1e30
SCALE = 1.0 / math.sqrt(HD)
SCALE2 = SCALE * math.log2(math.e)
MESH = pl.DeviceIdType.MESH


def remote(src, dst, send_sem, recv_sem, target):
    return pltpu.make_async_remote_copy(
        src_ref=src,
        dst_ref=dst,
        send_sem=send_sem,
        recv_sem=recv_sem,
        device_id={"ctx": target},
        device_id_type=MESH,
    )


def dot_nt(a, b):
    return lax.dot_general(a, b, (((1,), (1,)), ((), ())), preferred_element_type=jnp.float32)


def dot_nn(a, b):
    return jnp.dot(a, b, preferred_element_type=jnp.float32)


def dot_tn(a, b):
    return lax.dot_general(a, b, (((0,), (0,)), ((), ())), preferred_element_type=jnp.float32)


def kernel(
    n, first, far, len_ref, q_hbm, k_hbm, v_hbm, g_hbm,
    att_ref, dq_ref, dk_ref, dv_ref,
    q_ref, k_ref, v_ref, g_ref, kv_buf, qd_buf, rl_buf, pr_buf, pg_out, pg_buf, ld_own, ld_buf,
    s_buf, sp_buf, top_ref, tot_ref, out_t, dq_t,
    kv_ss, kv_rs, qd_ss, qd_rs, ld_ss, ld_rs, pr_ss, pr_rs, pg_ss, pg_rs, rl_ss, rl_rs, in_sem,
):
    rows, width = q_ref.shape
    heads = width // HD
    docs = len_ref.shape[0]
    me = lax.axis_index("ctx")
    later = n - first
    reach = max(far, first - 1)
    chunks = [pl.ds(c * PROMPT, PROMPT) for c in range(rows // PROMPT)]

    def has_before(d):
        near = (me >= d) & (me < first)
        return near | (me >= first + d) if d <= far else near

    def has_after(d):
        near = me + d < first
        return near | ((me >= first) & (me + d < n)) if d <= far else near

    own_copies = [
        pltpu.make_async_copy(src, dst, in_sem.at[i])
        for i, (src, dst) in enumerate(
            ((q_hbm, q_ref), (k_hbm, k_ref), (v_hbm, v_ref), (g_hbm, g_ref))
        )
    ]
    for copy in own_copies:
        copy.start()

    barrier = pltpu.get_barrier_semaphore()
    for s in range(1, n):
        pl.semaphore_signal(
            barrier, inc=1, device_id={"ctx": lax.rem(me + s, n)}, device_id_type=MESH
        )
    pl.semaphore_wait(barrier, n - 1)

    def kv_copy(d, w, c):
        src = (k_hbm, v_hbm)[w]
        return remote(
            src.at[chunks[c]], kv_buf.at[d - 1, w, chunks[c]],
            kv_ss.at[d - 1, w, c], kv_rs.at[d - 1, w, c], lax.rem(me + d, n),
        )

    def qd_copy(d, w, c):
        src = (q_hbm, g_hbm)[w]
        return remote(
            src.at[chunks[c]], qd_buf.at[d - 1, w, chunks[c]],
            qd_ss.at[d - 1, w, c], qd_rs.at[d - 1, w, c], lax.rem(me + n - d, n),
        )

    def qd_to_relay(w, c):
        src = (q_hbm, g_hbm)[w]
        return remote(
            src.at[chunks[c]], rl_buf.at[w, chunks[c]], qd_ss.at[0, w, c], rl_rs.at[w, c], first
        )

    def qd_relayed(w, c):
        return remote(
            rl_buf.at[w, chunks[c]], qd_buf.at[0, w, chunks[c]],
            rl_ss.at[w, c], qd_rs.at[0, w, c], first - 2,
        )

    parts = [(w, c) for c in range(len(chunks)) for w in (0, 1)]

    def ld_copy(d):
        return remote(
            ld_own, ld_buf.at[d - 1], ld_ss.at[d - 1], ld_rs.at[d - 1], lax.rem(me + n - d, n)
        )

    def pr_source(t):
        return (t + 1 - first % 2) % 2 if t < first + 4 else t - 4

    def pr_slot(t):
        return 0 if t >= first + 4 else (t - first) // 2

    def pr_copy(t, w):
        source = pr_source(t)
        if source == 0:
            src = (k_hbm, v_hbm)[w].at[chunks[0]]
        elif source == 1:
            src = kv_buf.at[0, w, chunks[0]]
        else:
            src = pr_buf.at[w]
        slot = pr_slot(t)
        return remote(src, pr_buf.at[w], pr_ss.at[slot, w], pr_rs.at[w], t)

    def pass_prompt(w):
        for t in range(first, n):
            @pl.when(me == pr_source(t))
            def _(t=t):
                pr_copy(t, w).start()

    def take_prompt():
        for w in (0, 1):
            remote(pr_buf.at[w], pr_buf.at[w], pr_ss.at[0, w], pr_rs.at[w], first).wait_recv()
            pass_prompt(w)

    def pg_copy():
        slot = lax.rem(me + n - first, n)
        return remote(pg_out, pg_buf.at[slot], pg_ss, pg_rs.at[slot], 0)

    distances = range(1, reach + 1)
    for c in range(len(chunks)):
        for d in distances:
            @pl.when(has_after(d))
            def _(d=d, c=c):
                for w in (0, 1):
                    kv_copy(d, w, c).start()
        if c == 0:
            @pl.when(me == 0)
            def _():
                for w in (0, 1):
                    pass_prompt(w)

    direct, by_relay = parts[: len(parts) // 2], parts[len(parts) // 2 :]

    @pl.when(me == first - 1)
    def _():
        for w, c in by_relay:
            qd_to_relay(w, c).start()
        for w, c in direct:
            qd_copy(1, w, c).start()

    def send_qd(d):
        for w, c in parts:
            qd_copy(d, w, c).start()

    for d in range(2, first):
        pl.when(me == first - 1)(functools.partial(send_qd, d))
    for d in range(1, first - 1):
        @pl.when((me >= d) & (me < first - 1))
        def _(d=d):
            send_qd(d)

    @pl.when(me == 1)
    def _():
        for w in (0, 1):
            kv_copy(1, w, 0).wait_recv()
            pass_prompt(w)

    @pl.when(me == first)
    def _():
        def relay(some):
            for w, c in some:
                remote(
                    rl_buf.at[w, chunks[c]], rl_buf.at[w, chunks[c]],
                    rl_ss.at[w, c], rl_rs.at[w, c], first - 1,
                ).wait_recv()
                qd_relayed(w, c).start()

        relay(by_relay[:2])
        take_prompt()
        relay(by_relay[2:])

    for copy in own_copies:
        copy.wait()

    def doc_start(pos):
        start = jnp.zeros_like(pos)
        end = jnp.int32(0)
        for i in range(docs):
            end = end + len_ref[i]
            start = jnp.where(pos >= end, end, start)
        return start

    u_pos = me * rows + lax.broadcasted_iota(jnp.int32, (rows, 1), 0)
    t_pos = me * rows + lax.broadcasted_iota(jnp.int32, (1, rows), 1)
    t_start = doc_start(t_pos)

    def hs(h):
        return pl.ds(h * HD, HD)

    def each_head(body):
        for h in range(heads):
            body(h)

    def forward(h, keys, values, mask):
        s = dot_nt(keys, q_ref[:, hs(h)]) * SCALE2
        if mask is not None:
            s = jnp.where(mask, s, NEG_FILL)
        top = top_ref[pl.ds(h, 1)]
        fresh = jnp.maximum(top, jnp.max(s, axis=0, keepdims=True))
        fade = jnp.exp2(top - fresh)
        p = jnp.exp2(s - fresh)
        top_ref[pl.ds(h, 1)] = fresh
        tot_ref[pl.ds(h, 1)] = tot_ref[pl.ds(h, 1)] * fade + jnp.sum(p, axis=0, keepdims=True)
        out_t[h] = out_t[h] * fade + dot_tn(values, p.astype(jnp.bfloat16))
        return s

    own_mask = (u_pos <= t_pos) & (u_pos >= t_start)

    @each_head
    def _(h):
        s = dot_nt(k_ref[:, hs(h)], q_ref[:, hs(h)]) * SCALE2
        s = jnp.where(own_mask, s, NEG_FILL)
        top = jnp.max(s, axis=0, keepdims=True)
        p = jnp.exp2(s - top)
        s_buf[0, h] = s
        top_ref[pl.ds(h, 1)] = top
        tot_ref[pl.ds(h, 1)] = jnp.sum(p, axis=0, keepdims=True)
        out_t[h] = dot_tn(v_ref[:, hs(h)], p.astype(jnp.bfloat16))

    @pl.when(me > first)
    def _():
        take_prompt()

    @pl.when(me >= first)
    def _():
        @each_head
        def _(h):
            sp_buf[h] = forward(h, pr_buf[0, :, hs(h)], pr_buf[1, :, hs(h)], None)

    for d in range(1, far + 1):
        @pl.when(me >= first + d)
        def _(d=d):
            send_qd(d)

    for d in distances:
        @pl.when(has_before(d))
        def _(d=d):
            for w, c in parts:
                if c == 0 and d == 1:
                    @pl.when(me != 1)
                    def _(w=w):
                        kv_copy(1, w, 0).wait_recv()
                else:
                    kv_copy(d, w, c).wait_recv()
            mask = u_pos - d * rows >= t_start

            @each_head
            def _(h):
                s_buf[d, h] = forward(
                    h, kv_buf[d - 1, 0, :, hs(h)], kv_buf[d - 1, 1, :, hs(h)], mask
                )

    @each_head
    def _(h):
        total = tot_ref[pl.ds(h, 1)]
        out = out_t[h] / total
        att_ref[:, hs(h)] = jnp.transpose(out)
        grad = jnp.transpose(g_ref[:, hs(h)].astype(jnp.float32))
        ld_own[pl.ds(h, 1)] = top_ref[pl.ds(h, 1)] + jnp.log2(total)
        ld_own[pl.ds(heads + h, 1)] = jnp.sum(out * grad, axis=0, keepdims=True)

    for d in distances:
        @pl.when(has_before(d))
        def _(d=d):
            ld_copy(d).start()

    def backward(s, g, lse, delta, values):
        p = jnp.exp2(s - lse)
        dp = dot_nt(values, g)
        return p.astype(jnp.bfloat16), (p * (dp - delta)).astype(jnp.bfloat16)

    def own_backward(h, s, values):
        return backward(
            s, g_ref[:, hs(h)], ld_own[pl.ds(h, 1)], ld_own[pl.ds(heads + h, 1)], values
        )

    @pl.when(me >= first)
    def _():
        @each_head
        def _(h):
            p, ds = own_backward(h, sp_buf[h], pr_buf[1, :, hs(h)])
            pg_out[0, :, hs(h)] = dot_nn(ds, q_ref[:, hs(h)]).astype(jnp.bfloat16)
            pg_out[1, :, hs(h)] = dot_nn(p, g_ref[:, hs(h)]).astype(jnp.bfloat16)
            dq_t[h] = dot_tn(pr_buf[0, :, hs(h)], ds)

        pg_copy().start()

    @pl.when(me < first)
    def _():
        dq_t[...] = jnp.zeros_like(dq_t)

    @each_head
    def _(h):
        p, ds = own_backward(h, s_buf[0, h], v_ref[:, hs(h)])
        dk_ref[:, hs(h)] = dot_nn(ds, q_ref[:, hs(h)])
        dv_ref[:, hs(h)] = dot_nn(p, g_ref[:, hs(h)])
        dq_t[h] += dot_tn(k_ref[:, hs(h)], ds)

    for d in distances:
        @pl.when(has_before(d))
        def _(d=d):
            @each_head
            def _(h):
                p, ds = own_backward(h, s_buf[d, h], kv_buf[d - 1, 1, :, hs(h)])
                dq_t[h] += dot_tn(kv_buf[d - 1, 0, :, hs(h)], ds)

    @each_head
    def _(h):
        dq_ref[:, hs(h)] = jnp.transpose(dq_t[h] * SCALE)

    for d in distances:
        @pl.when(has_after(d))
        def _(d=d):
            for w, c in parts:
                qd_copy(d, w, c).wait_recv()
            ld_copy(d).wait_recv()
            mask = u_pos >= doc_start(t_pos + d * rows)

            @each_head
            def _(h):
                q = qd_buf[d - 1, 0, :, hs(h)]
                g = qd_buf[d - 1, 1, :, hs(h)]
                s = jnp.where(mask, dot_nt(k_ref[:, hs(h)], q) * SCALE2, NEG_FILL)
                p, ds = backward(
                    s, g, ld_buf[d - 1, pl.ds(h, 1)], ld_buf[d - 1, pl.ds(heads + h, 1)],
                    v_ref[:, hs(h)],
                )
                dk_ref[:, hs(h)] += dot_nn(ds, q)
                dv_ref[:, hs(h)] += dot_nn(p, g)

    @pl.when(me == 0)
    def _():
        @pl.loop(0, later)
        def _(i):
            remote(pg_out, pg_buf.at[i], pg_ss, pg_rs.at[i], 0).wait_recv()
            dk_ref[pl.ds(0, PROMPT)] += pg_buf[i, 0].astype(jnp.float32)
            dv_ref[pl.ds(0, PROMPT)] += pg_buf[i, 1].astype(jnp.float32)

    dk_ref[...] = dk_ref[...] * SCALE

    for d in distances:
        @pl.when(has_after(d))
        def _(d=d):
            for w, c in parts:
                kv_copy(d, w, c).wait_send()

        @pl.when(has_before(d))
        def _(d=d):
            for w, c in parts:
                qd_copy(d, w, c).wait_send()
            ld_copy(d).wait_send()

    @pl.when(me == first)
    def _():
        for w, c in by_relay:
            qd_relayed(w, c).wait_send()

    for t in range(first, n):
        @pl.when(me == pr_source(t))
        def _(t=t):
            for w in (0, 1):
                pr_copy(t, w).wait_send()

    @pl.when(me >= first)
    def _():
        pg_copy().wait_send()


def attention(far, queries, keys, values, out_grad, doc_lengths):
    rows, width = queries.shape
    heads = width // HD
    n = lax.axis_size("ctx")
    first = DOC_MOST // rows
    later = n - first
    reach = max(far, first - 1)
    cuts = rows // PROMPT
    bf, f32 = jnp.bfloat16, jnp.float32
    vmem = pl.BlockSpec(memory_space=pltpu.VMEM)
    hbm = pl.BlockSpec(memory_space=pltpu.HBM)
    dma = pltpu.SemaphoreType.DMA
    tile = rows * rows * heads
    out = jax.ShapeDtypeStruct((rows, width), f32)
    return pl.pallas_call(
        functools.partial(kernel, n, first, far),
        out_shape=[out] * 4,
        in_specs=[pl.BlockSpec(memory_space=pltpu.SMEM)] + [hbm] * 4,
        out_specs=[vmem] * 4,
        scratch_shapes=[pltpu.VMEM((rows, width), bf)] * 4
        + [
            pltpu.VMEM((reach, 2, rows, width), bf),
            pltpu.VMEM((reach, 2, rows, width), bf),
            pltpu.VMEM((2, rows, width), bf),
            pltpu.VMEM((2, PROMPT, width), bf),
            pltpu.VMEM((2, PROMPT, width), bf),
            pltpu.VMEM((later, 2, PROMPT, width), bf),
            pltpu.VMEM((2 * heads, rows), f32),
            pltpu.VMEM((reach, 2 * heads, rows), f32),
            pltpu.VMEM((reach + 1, heads, rows, rows), f32),
            pltpu.VMEM((heads, PROMPT, rows), f32),
            pltpu.VMEM((heads, rows), f32),
            pltpu.VMEM((heads, rows), f32),
            pltpu.VMEM((heads, HD, rows), f32),
            pltpu.VMEM((heads, HD, rows), f32),
            dma((reach, 2, cuts)), dma((reach, 2, cuts)),
            dma((reach, 2, cuts)), dma((reach, 2, cuts)),
            dma((reach,)), dma((reach,)),
            dma((2, 2)), dma((2,)),
            dma(()), dma((later,)),
            dma((2, cuts)), dma((2, cuts)), dma((4,)),
        ],
        compiler_params=pltpu.CompilerParams(
            collective_id=far, has_side_effects=True, vmem_limit_bytes=48 * 2**20
        ),
        cost_estimate=pl.CostEstimate(
            flops=2 * 8 * 4 * tile * HD, bytes_accessed=12 * rows * width, transcendentals=8 * tile
        ),
    )(doc_lengths, queries, keys, values, out_grad)


def write_kernel(*refs):
    count = len(refs) // 2
    copies = []
    for i in range(count):
        half = refs[i].shape[0] // 2
        for j in (0, 1):
            part = pl.ds(j * half, half)
            copies.append(
                pltpu.make_async_copy(
                    refs[i].at[part], refs[count + i].at[part], refs[-1].at[i, j]
                )
            )
    for copy in copies:
        copy.start()
    for copy in copies:
        copy.wait()


def written(arrays):
    hbm = pl.BlockSpec(memory_space=pltpu.HBM)
    return pl.pallas_call(
        write_kernel,
        out_shape=[jax.ShapeDtypeStruct(a.shape, a.dtype) for a in arrays],
        in_specs=[pl.BlockSpec(memory_space=pl.ANY)] * len(arrays),
        out_specs=[hbm] * len(arrays),
        scratch_shapes=[pltpu.SemaphoreType.DMA((len(arrays), 2))],
        compiler_params=pltpu.CompilerParams(vmem_limit_bytes=2**20),
    )(*arrays)


def on_device(queries, keys, values, out_grad, doc_lengths):
    rows = queries.shape[0]
    docs = doc_lengths.shape[0]
    order = jnp.arange(docs)
    ends = jnp.sum(jnp.where(order[:, None] <= order[None, :], doc_lengths[:, None], 0), axis=0)
    span = (ends - 1) // rows - (ends - doc_lengths) // rows
    far = jnp.any((span > 1) & (order > 0))
    arrays = lax.cond(
        far,
        functools.partial(attention, REACH),
        functools.partial(attention, 1),
        queries, keys, values, out_grad, doc_lengths,
    )
    return tuple(written(arrays))


def solution(mesh):
    block = P("ctx", "head")
    return jax.shard_map(
        on_device, mesh=mesh, in_specs=(block,) * 4 + (P(),), out_specs=(block,) * 4, check_vma=False
    )
```

```python
import functools
import math

import jax
import jax.numpy as jnp
from jax import lax
from jax.experimental import pallas as pl
from jax.experimental.pallas import tpu as pltpu
from jax.sharding import PartitionSpec as P

HD = 128
PROMPT = 64
DOC_MOST = 768
REACH = 3
NEG_FILL = -1e30
SCALE = 1.0 / math.sqrt(HD)
SCALE2 = SCALE * math.log2(math.e)
MESH = pl.DeviceIdType.MESH


def remote(src, dst, send_sem, recv_sem, target):
    return pltpu.make_async_remote_copy(
        src_ref=src,
        dst_ref=dst,
        send_sem=send_sem,
        recv_sem=recv_sem,
        device_id={"ctx": target},
        device_id_type=MESH,
    )


def dot_nt(a, b):
    return lax.dot_general(a, b, (((1,), (1,)), ((), ())), preferred_element_type=jnp.float32)


def dot_nn(a, b):
    return jnp.dot(a, b, preferred_element_type=jnp.float32)


def dot_tn(a, b):
    return lax.dot_general(a, b, (((0,), (0,)), ((), ())), preferred_element_type=jnp.float32)


def kernel(
    n, first, far, len_ref, q_hbm, k_hbm, v_hbm, g_hbm,
    att_ref, dq_ref, dk_ref, dv_ref,
    q_ref, k_ref, v_ref, g_ref, kv_buf, qd_buf, rl_buf, pr_buf, pg_out, pg_buf, ld_own, ld_buf,
    s_buf, sp_buf, top_ref, tot_ref, out_t, dq_t,
    kv_ss, kv_rs, qd_ss, qd_rs, ld_ss, ld_rs, pr_ss, pr_rs, pg_ss, pg_rs, rl_ss, rl_rs, in_sem,
):
    rows, width = q_ref.shape
    heads = width // HD
    docs = len_ref.shape[0]
    me = lax.axis_index("ctx")
    later = n - first
    reach = max(far, first - 1)
    chunks = [pl.ds(c * PROMPT, PROMPT) for c in range(rows // PROMPT)]

    def has_before(d):
        near = (me >= d) & (me < first)
        return near | (me >= first + d) if d <= far else near

    def has_after(d):
        near = me + d < first
        return near | ((me >= first) & (me + d < n)) if d <= far else near

    own_copies = [
        pltpu.make_async_copy(src, dst, in_sem.at[i])
        for i, (src, dst) in enumerate(
            ((q_hbm, q_ref), (k_hbm, k_ref), (v_hbm, v_ref), (g_hbm, g_ref))
        )
    ]
    for copy in own_copies:
        copy.start()

    barrier = pltpu.get_barrier_semaphore()
    for s in range(1, n):
        pl.semaphore_signal(
            barrier, inc=1, device_id={"ctx": lax.rem(me + s, n)}, device_id_type=MESH
        )
    pl.semaphore_wait(barrier, n - 1)

    def kv_copy(d, w, c):
        src = (k_hbm, v_hbm)[w]
        return remote(
            src.at[chunks[c]], kv_buf.at[d - 1, w, chunks[c]],
            kv_ss.at[d - 1, w, c], kv_rs.at[d - 1, w, c], lax.rem(me + d, n),
        )

    def qd_copy(d, w, c):
        src = (q_hbm, g_hbm)[w]
        return remote(
            src.at[chunks[c]], qd_buf.at[d - 1, w, chunks[c]],
            qd_ss.at[d - 1, w, c], qd_rs.at[d - 1, w, c], lax.rem(me + n - d, n),
        )

    def qd_to_relay(w, c):
        src = (q_hbm, g_hbm)[w]
        return remote(
            src.at[chunks[c]], rl_buf.at[w, chunks[c]], qd_ss.at[0, w, c], rl_rs.at[w, c], first
        )

    def qd_relayed(w, c):
        return remote(
            rl_buf.at[w, chunks[c]], qd_buf.at[0, w, chunks[c]],
            rl_ss.at[w, c], qd_rs.at[0, w, c], first - 2,
        )

    parts = [(w, c) for c in range(len(chunks)) for w in (0, 1)]

    def ld_copy(d):
        return remote(
            ld_own, ld_buf.at[d - 1], ld_ss.at[d - 1], ld_rs.at[d - 1], lax.rem(me + n - d, n)
        )

    def pr_source(t):
        return (t + 1 - first % 2) % 2 if t < first + 4 else t - 4

    def pr_slot(t):
        return 0 if t >= first + 4 else (t - first) // 2

    def pr_copy(t, w):
        source = pr_source(t)
        if source == 0:
            src = (k_hbm, v_hbm)[w].at[chunks[0]]
        elif source == 1:
            src = kv_buf.at[0, w, chunks[0]]
        else:
            src = pr_buf.at[w]
        slot = pr_slot(t)
        return remote(src, pr_buf.at[w], pr_ss.at[slot, w], pr_rs.at[w], t)

    def pass_prompt(w):
        for t in range(first, n):
            @pl.when(me == pr_source(t))
            def _(t=t):
                pr_copy(t, w).start()

    def take_prompt():
        for w in (0, 1):
            remote(pr_buf.at[w], pr_buf.at[w], pr_ss.at[0, w], pr_rs.at[w], first).wait_recv()
            pass_prompt(w)

    def pg_copy():
        slot = lax.rem(me + n - first, n)
        return remote(pg_out, pg_buf.at[slot], pg_ss, pg_rs.at[slot], 0)

    distances = range(1, reach + 1)
    for c in range(len(chunks)):
        for d in distances:
            @pl.when(has_after(d))
            def _(d=d, c=c):
                for w in (0, 1):
                    kv_copy(d, w, c).start()
        if c == 0:
            @pl.when(me == 0)
            def _():
                for w in (0, 1):
                    pass_prompt(w)

    direct, by_relay = parts[: len(parts) // 2], parts[len(parts) // 2 :]

    @pl.when(me == first - 1)
    def _():
        for w, c in by_relay:
            qd_to_relay(w, c).start()
        for w, c in direct:
            qd_copy(1, w, c).start()

    def send_qd(d):
        for w, c in parts:
            qd_copy(d, w, c).start()

    for d in range(2, first):
        pl.when(me == first - 1)(functools.partial(send_qd, d))
    for d in range(1, first - 1):
        @pl.when((me >= d) & (me < first - 1))
        def _(d=d):
            send_qd(d)

    @pl.when(me == 1)
    def _():
        for w in (0, 1):
            kv_copy(1, w, 0).wait_recv()
            pass_prompt(w)

    @pl.when(me == first)
    def _():
        def relay(some):
            for w, c in some:
                remote(
                    rl_buf.at[w, chunks[c]], rl_buf.at[w, chunks[c]],
                    rl_ss.at[w, c], rl_rs.at[w, c], first - 1,
                ).wait_recv()
                qd_relayed(w, c).start()

        relay(by_relay[:2])
        take_prompt()
        relay(by_relay[2:])

    for copy in own_copies:
        copy.wait()

    def doc_start(pos):
        start = jnp.zeros_like(pos)
        end = jnp.int32(0)
        for i in range(docs):
            end = end + len_ref[i]
            start = jnp.where(pos >= end, end, start)
        return start

    u_pos = me * rows + lax.broadcasted_iota(jnp.int32, (rows, 1), 0)
    t_pos = me * rows + lax.broadcasted_iota(jnp.int32, (1, rows), 1)
    t_start = doc_start(t_pos)

    def hs(h):
        return pl.ds(h * HD, HD)

    def each_head(body):
        for h in range(heads):
            body(h)

    def forward(h, keys, values, mask):
        s = dot_nt(keys, q_ref[:, hs(h)]) * SCALE2
        if mask is not None:
            s = jnp.where(mask, s, NEG_FILL)
        top = top_ref[pl.ds(h, 1)]
        fresh = jnp.maximum(top, jnp.max(s, axis=0, keepdims=True))
        fade = jnp.exp2(top - fresh)
        p = jnp.exp2(s - fresh)
        top_ref[pl.ds(h, 1)] = fresh
        tot_ref[pl.ds(h, 1)] = tot_ref[pl.ds(h, 1)] * fade + jnp.sum(p, axis=0, keepdims=True)
        out_t[h] = out_t[h] * fade + dot_tn(values, p.astype(jnp.bfloat16))
        return s

    own_mask = (u_pos <= t_pos) & (u_pos >= t_start)

    @each_head
    def _(h):
        s = dot_nt(k_ref[:, hs(h)], q_ref[:, hs(h)]) * SCALE2
        s = jnp.where(own_mask, s, NEG_FILL)
        top = jnp.max(s, axis=0, keepdims=True)
        p = jnp.exp2(s - top)
        s_buf[0, h] = s
        top_ref[pl.ds(h, 1)] = top
        tot_ref[pl.ds(h, 1)] = jnp.sum(p, axis=0, keepdims=True)
        out_t[h] = dot_tn(v_ref[:, hs(h)], p.astype(jnp.bfloat16))

    for d in range(1, far + 1):
        @pl.when(me >= first + d)
        def _(d=d):
            send_qd(d)

    @pl.when(me > first)
    def _():
        take_prompt()

    @pl.when(me >= first)
    def _():
        @each_head
        def _(h):
            sp_buf[h] = forward(h, pr_buf[0, :, hs(h)], pr_buf[1, :, hs(h)], None)

    for d in distances:
        @pl.when(has_before(d))
        def _(d=d):
            for w, c in parts:
                if c == 0 and d == 1:
                    @pl.when(me != 1)
                    def _(w=w):
                        kv_copy(1, w, 0).wait_recv()
                else:
                    kv_copy(d, w, c).wait_recv()
            mask = u_pos - d * rows >= t_start

            @each_head
            def _(h):
                s_buf[d, h] = forward(
                    h, kv_buf[d - 1, 0, :, hs(h)], kv_buf[d - 1, 1, :, hs(h)], mask
                )

    @each_head
    def _(h):
        total = tot_ref[pl.ds(h, 1)]
        out = out_t[h] / total
        att_ref[:, hs(h)] = jnp.transpose(out)
        grad = jnp.transpose(g_ref[:, hs(h)].astype(jnp.float32))
        ld_own[pl.ds(h, 1)] = top_ref[pl.ds(h, 1)] + jnp.log2(total)
        ld_own[pl.ds(heads + h, 1)] = jnp.sum(out * grad, axis=0, keepdims=True)

    for d in distances:
        @pl.when(has_before(d))
        def _(d=d):
            ld_copy(d).start()

    def backward(s, g, lse, delta, values):
        p = jnp.exp2(s - lse)
        dp = dot_nt(values, g)
        return p.astype(jnp.bfloat16), (p * (dp - delta)).astype(jnp.bfloat16)

    def own_backward(h, s, values):
        return backward(
            s, g_ref[:, hs(h)], ld_own[pl.ds(h, 1)], ld_own[pl.ds(heads + h, 1)], values
        )

    @pl.when(me >= first)
    def _():
        @each_head
        def _(h):
            p, ds = own_backward(h, sp_buf[h], pr_buf[1, :, hs(h)])
            pg_out[0, :, hs(h)] = dot_nn(ds, q_ref[:, hs(h)]).astype(jnp.bfloat16)
            pg_out[1, :, hs(h)] = dot_nn(p, g_ref[:, hs(h)]).astype(jnp.bfloat16)
            dq_t[h] = dot_tn(pr_buf[0, :, hs(h)], ds)

        pg_copy().start()

    @pl.when(me < first)
    def _():
        dq_t[...] = jnp.zeros_like(dq_t)

    @each_head
    def _(h):
        p, ds = own_backward(h, s_buf[0, h], v_ref[:, hs(h)])
        dk_ref[:, hs(h)] = dot_nn(ds, q_ref[:, hs(h)])
        dv_ref[:, hs(h)] = dot_nn(p, g_ref[:, hs(h)])
        dq_t[h] += dot_tn(k_ref[:, hs(h)], ds)

    for d in distances:
        @pl.when(has_before(d))
        def _(d=d):
            @each_head
            def _(h):
                p, ds = own_backward(h, s_buf[d, h], kv_buf[d - 1, 1, :, hs(h)])
                dq_t[h] += dot_tn(kv_buf[d - 1, 0, :, hs(h)], ds)

    @each_head
    def _(h):
        dq_ref[:, hs(h)] = jnp.transpose(dq_t[h] * SCALE)

    for d in distances:
        @pl.when(has_after(d))
        def _(d=d):
            for w, c in parts:
                qd_copy(d, w, c).wait_recv()
            ld_copy(d).wait_recv()
            mask = u_pos >= doc_start(t_pos + d * rows)

            @each_head
            def _(h):
                q = qd_buf[d - 1, 0, :, hs(h)]
                g = qd_buf[d - 1, 1, :, hs(h)]
                s = jnp.where(mask, dot_nt(k_ref[:, hs(h)], q) * SCALE2, NEG_FILL)
                p, ds = backward(
                    s, g, ld_buf[d - 1, pl.ds(h, 1)], ld_buf[d - 1, pl.ds(heads + h, 1)],
                    v_ref[:, hs(h)],
                )
                dk_ref[:, hs(h)] += dot_nn(ds, q)
                dv_ref[:, hs(h)] += dot_nn(p, g)

    @pl.when(me == 0)
    def _():
        @pl.loop(0, later)
        def _(i):
            remote(pg_out, pg_buf.at[i], pg_ss, pg_rs.at[i], 0).wait_recv()
            dk_ref[pl.ds(0, PROMPT)] += pg_buf[i, 0].astype(jnp.float32)
            dv_ref[pl.ds(0, PROMPT)] += pg_buf[i, 1].astype(jnp.float32)

    dk_ref[...] = dk_ref[...] * SCALE

    for d in distances:
        @pl.when(has_after(d))
        def _(d=d):
            for w, c in parts:
                kv_copy(d, w, c).wait_send()

        @pl.when(has_before(d))
        def _(d=d):
            for w, c in parts:
                qd_copy(d, w, c).wait_send()
            ld_copy(d).wait_send()

    @pl.when(me == first)
    def _():
        for w, c in by_relay:
            qd_relayed(w, c).wait_send()

    for t in range(first, n):
        @pl.when(me == pr_source(t))
        def _(t=t):
            for w in (0, 1):
                pr_copy(t, w).wait_send()

    @pl.when(me >= first)
    def _():
        pg_copy().wait_send()


def attention(far, queries, keys, values, out_grad, doc_lengths):
    rows, width = queries.shape
    heads = width // HD
    n = lax.axis_size("ctx")
    first = DOC_MOST // rows
    later = n - first
    reach = max(far, first - 1)
    cuts = rows // PROMPT
    bf, f32 = jnp.bfloat16, jnp.float32
    vmem = pl.BlockSpec(memory_space=pltpu.VMEM)
    hbm = pl.BlockSpec(memory_space=pltpu.HBM)
    dma = pltpu.SemaphoreType.DMA
    tile = rows * rows * heads
    out = jax.ShapeDtypeStruct((rows, width), f32)
    return pl.pallas_call(
        functools.partial(kernel, n, first, far),
        out_shape=[out] * 4,
        in_specs=[pl.BlockSpec(memory_space=pltpu.SMEM)] + [hbm] * 4,
        out_specs=[vmem] * 4,
        scratch_shapes=[pltpu.VMEM((rows, width), bf)] * 4
        + [
            pltpu.VMEM((reach, 2, rows, width), bf),
            pltpu.VMEM((reach, 2, rows, width), bf),
            pltpu.VMEM((2, rows, width), bf),
            pltpu.VMEM((2, PROMPT, width), bf),
            pltpu.VMEM((2, PROMPT, width), bf),
            pltpu.VMEM((later, 2, PROMPT, width), bf),
            pltpu.VMEM((2 * heads, rows), f32),
            pltpu.VMEM((reach, 2 * heads, rows), f32),
            pltpu.VMEM((reach + 1, heads, rows, rows), f32),
            pltpu.VMEM((heads, PROMPT, rows), f32),
            pltpu.VMEM((heads, rows), f32),
            pltpu.VMEM((heads, rows), f32),
            pltpu.VMEM((heads, HD, rows), f32),
            pltpu.VMEM((heads, HD, rows), f32),
            dma((reach, 2, cuts)), dma((reach, 2, cuts)),
            dma((reach, 2, cuts)), dma((reach, 2, cuts)),
            dma((reach,)), dma((reach,)),
            dma((2, 2)), dma((2,)),
            dma(()), dma((later,)),
            dma((2, cuts)), dma((2, cuts)), dma((4,)),
        ],
        compiler_params=pltpu.CompilerParams(
            collective_id=far, has_side_effects=True, vmem_limit_bytes=48 * 2**20
        ),
        cost_estimate=pl.CostEstimate(
            flops=2 * 8 * 4 * tile * HD, bytes_accessed=12 * rows * width, transcendentals=8 * tile
        ),
    )(doc_lengths, queries, keys, values, out_grad)


def write_kernel(*refs):
    count = len(refs) // 2
    copies = []
    for i in range(count):
        half = refs[i].shape[0] // 2
        for j in (0, 1):
            part = pl.ds(j * half, half)
            copies.append(
                pltpu.make_async_copy(
                    refs[i].at[part], refs[count + i].at[part], refs[-1].at[i, j]
                )
            )
    for copy in copies:
        copy.start()
    for copy in copies:
        copy.wait()


def written(arrays):
    hbm = pl.BlockSpec(memory_space=pltpu.HBM)
    return pl.pallas_call(
        write_kernel,
        out_shape=[jax.ShapeDtypeStruct(a.shape, a.dtype) for a in arrays],
        in_specs=[pl.BlockSpec(memory_space=pl.ANY)] * len(arrays),
        out_specs=[hbm] * len(arrays),
        scratch_shapes=[pltpu.SemaphoreType.DMA((len(arrays), 2))],
        compiler_params=pltpu.CompilerParams(vmem_limit_bytes=2**20),
    )(*arrays)


def on_device(queries, keys, values, out_grad, doc_lengths):
    rows = queries.shape[0]
    docs = doc_lengths.shape[0]
    order = jnp.arange(docs)
    ends = jnp.sum(jnp.where(order[:, None] <= order[None, :], doc_lengths[:, None], 0), axis=0)
    span = (ends - 1) // rows - (ends - doc_lengths) // rows
    far = jnp.any((span > 1) & (order > 0))
    arrays = lax.cond(
        far,
        functools.partial(attention, REACH),
        functools.partial(attention, 1),
        queries, keys, values, out_grad, doc_lengths,
    )
    return tuple(written(arrays))


def solution(mesh):
    block = P("ctx", "head")
    return jax.shard_map(
        on_device, mesh=mesh, in_specs=(block,) * 4 + (P(),), out_specs=(block,) * 4, check_vma=False
    )
```
